32 devices in a mesh: row: 8 (over y, x, core), col: 4 (over z).
Axes of the slice: x: 2, y: 2, z: 4, core: 2. Of those that a mesh axis runs over, the one named last changes fastest.
Arguments:
- trial: float32 [1, 256, 1024], P(None, None, 'row'), may hold values from -6 to 6
- screened: bfloat16 [768, 768], P('row', 'col'), may hold values from -4 to 4
- val_points: bfloat16 [768, 256], P('row'), may hold values from -0.375 to 0.375
- cond_points: bfloat16 [768, 1024], P('col', 'row'), may hold values from -0.1875 to 0.1875
- eps_val: float32 [256], replicated, may hold values from -0.6 to -0.1
- eps_cond: float32 [1024], replicated, may hold values from 0.1 to 1
Outputs:
- applied: float32 [1, 256, 1024], P(None, None, 'row')
The draws below stay inside these ranges and needn't reach their ends.
All inputs are finite; a program needn't handle non-finite values.
Results may differ from the reference program's by a relative error of at most 0.02.
Values may be sent and summed in bfloat16 or wider, within the bound.
A program may use at most 64 MiB of HBM per device.

```python
import jax
import jax.numpy as jnp
from jax import lax

NV = 256
NC = 1024
NB = 1
APPLY = 2
P_SIZE = 768
N_ROW = 8
N_COL = 4


def block_levels(key, extent, pieces, least, top_value):
    gain = 1.0
    for dim, parts in pieces:
        steps = jax.random.uniform(jax.random.fold_in(jax.random.fold_in(key, 6), dim), (parts,), jnp.float32, least / len(pieces), top_value / len(pieces))
        gain = gain * jnp.repeat(jnp.exp(steps), extent[dim] // parts).reshape((-1,) + (1,) * (len(extent) - 1 - dim))
    return gain


def gaussian(rng, dims, width, bound, shards=(), held_as=jnp.bfloat16):
    drawn = jax.random.normal(rng, dims, jnp.float32) * width
    if len(shards) > 0:
        drawn = block_levels(rng, dims, shards, -0.22, 0.18) * drawn
    return jnp.clip(drawn, min=-bound, max=bound).astype(held_as)


def setup_inputs(seed: int = 0) -> dict:
    arg_keys = jax.random.split(jax.random.key(seed), 7)
    trial = gaussian(arg_keys[0], (NB, NV, NC), 1.0, 6.0, ((2, 8),), jnp.float32)
    screened = gaussian(arg_keys[1], (P_SIZE, P_SIZE), (P_SIZE * P_SIZE // (NV * NC)) ** -0.5, 4.0, ((0, 8), (1, 4)))
    val_points = gaussian(arg_keys[2], (P_SIZE, NV), NV ** -0.5, 0.375, ((0, 8),))
    cond_points = gaussian(arg_keys[3], (P_SIZE, NC), NC ** -0.5, 0.1875, ((0, 4), (1, 8)))
    eps_val = jnp.clip(jax.random.uniform(arg_keys[4], (NV,), jnp.float32, -0.6, -0.1), -0.6, -0.1)
    eps_cond = jnp.clip(jax.random.uniform(arg_keys[5], (NC,), jnp.float32, 0.1, 1.0), 0.1, 1.0)
    return dict(trial=trial, screened=screened, val_points=val_points, cond_points=cond_points, eps_val=eps_val, eps_cond=eps_cond)


def reference(trial, screened, val_points, cond_points, eps_val, eps_cond):
    energy = eps_cond[None, :] - eps_val[:, None]
    block = P_SIZE // N_ROW
    cblock = P_SIZE // N_COL
    cond_wide = cond_points.astype(jnp.float32)
    val_wide = val_points.astype(jnp.float32)
    current = trial
    for step in range(APPLY):
        xb = current.astype(jnp.bfloat16)
        pair = jnp.einsum('mv,bvc->bmc', val_wide, xb.astype(jnp.float32)).astype(jnp.bfloat16)

        def one_block(total, index):
            start = (index * block).astype(jnp.int32)
            pair_blk = lax.dynamic_slice_in_dim(pair, start, block, 1).astype(jnp.float32)
            screen_blk = lax.dynamic_slice_in_dim(screened, start, block, 0).astype(jnp.float32)
            val_blk = lax.dynamic_slice_in_dim(val_wide, start, block, 0)
            inner = jnp.einsum('bmc,nc->bmn', pair_blk, cond_wide)
            tile = (screen_blk[None] * inner).astype(jnp.bfloat16)

            def one_column(acc, jindex):
                cstart = (jindex * cblock).astype(jnp.int32)
                tile_col = lax.dynamic_slice_in_dim(tile, cstart, cblock, 2).astype(jnp.float32)
                cond_col = lax.dynamic_slice_in_dim(cond_wide, cstart, cblock, 0)
                back = jnp.einsum('bmn,nc->bmc', tile_col, cond_col).astype(jnp.bfloat16)
                term = jnp.einsum('mv,bmc->bvc', val_blk, back.astype(jnp.float32)).astype(jnp.bfloat16)
                return acc + term.astype(jnp.float32), None

            total, _ = lax.scan(one_column, total, jnp.arange(N_COL, dtype=jnp.int32))
            return total, None

        kernel, _ = lax.scan(one_block, jnp.zeros((NB, NV, NC), jnp.float32), jnp.arange(N_ROW, dtype=jnp.int32))
        current = energy[None] * current + kernel
    return current
```

```python
import functools

import jax
import jax.numpy as jnp
from jax import lax
from jax.experimental import pallas as pl
from jax.experimental.pallas import tpu as pltpu
from jax.sharding import PartitionSpec as P

APPLY = 2
LANES = 128
ROWS16 = 16
F32 = jnp.float32
BF16 = jnp.bfloat16
MESH = pl.DeviceIdType.MESH


def dot_nt(a, b):
    return lax.dot_general(a, b, (((1,), (1,)), ((), ())), preferred_element_type=F32)


def dot_tn(a, b):
    return lax.dot_general(a, b, (((0,), (0,)), ((), ())), preferred_element_type=F32)


def kernel(nr, nj, x_ref, s_ref, v_ref, c_ref, ev_ref, ec_ref, out_ref,
           vall, st, sall, asend, arecv, craw, clo, chi, evb,
           ysend0, ysend1, yall0, yall1, esend, erecv, zsend, zrecv, kz0, kz1,
           row_send, row_recv, col_send, col_recv):
    r = lax.axis_index("row")
    j = lax.axis_index("col")
    mb, nv = v_ref.shape
    nb, cw = c_ref.shape
    nk = nb // nr
    slot = st.shape[1]
    half = slot // 2
    vj = nv // nj
    row_peers = [lax.rem(r + k, nr) for k in range(1, nr)]
    col_peers = [lax.rem(j + k, nj) for k in range(1, nj)]

    barrier = pltpu.get_barrier_semaphore()
    for s in row_peers:
        pl.semaphore_signal(barrier, inc=1, device_id=(s, j), device_id_type=MESH)
    for s in col_peers:
        pl.semaphore_signal(barrier, inc=1, device_id=(r, s), device_id_type=MESH)

    def row_copy(phase, src, dst, peer, slot_id):
        return pltpu.make_async_remote_copy(
            src_ref=src, dst_ref=dst, send_sem=row_send.at[phase, peer],
            recv_sem=row_recv.at[phase, slot_id], device_id=(peer, j), device_id_type=MESH)

    def col_copy(phase, src, dst, peer, slot_id):
        return pltpu.make_async_remote_copy(
            src_ref=src, dst_ref=dst, send_sem=col_send.at[phase, peer],
            recv_sem=col_recv.at[phase, slot_id], device_id=(r, peer), device_id_type=MESH)

    pending = []

    def row_start(phase, src_of, dst_of):
        for s in row_peers:
            copy = row_copy(phase, src_of(s), dst_of(r), s, r)
            copy.start()
            pending.append(copy)

    def row_wait(phase, dst_of):
        for s in reversed(row_peers):
            row_copy(phase, dst_of(s), dst_of(s), s, s).wait_recv()

    def col_start(phase, src_of, dst_of):
        for s in col_peers:
            copy = col_copy(phase, src_of(s), dst_of(j), s, j)
            copy.start()
            pending.append(copy)

    def col_wait(phase, dst_of):
        for s in col_peers:
            col_copy(phase, dst_of(s), dst_of(s), s, s).wait_recv()

    pad_rows = jnp.zeros((slot - nk, cw), F32)

    def padded(ref):
        wide = ref[...].astype(F32)
        return [
            jnp.concatenate([wide[i * nk:(i + 1) * nk], pad_rows], axis=0).astype(BF16)
            for i in range(nr)
        ]

    def place(blocks, col):
        for i, block in enumerate(blocks):
            clo[i, col] = block[:half]
            chi[i, col] = block[half:]

    own = padded(c_ref)
    first = dot_nt(jnp.concatenate(own, axis=0), x_ref[0].astype(BF16))
    for i in range(nr):
        asend[i] = first[i * slot:(i + 1) * slot].astype(BF16)
    arecv[r] = asend[r]

    pl.semaphore_wait(barrier, nr - 1 + nj - 1)
    row_start(0, lambda s: asend.at[s], lambda s: arecv.at[s])
    row_start(1, lambda s: v_ref, lambda s: vall.at[s, pl.ds(0, mb)])
    col_start(0, lambda s: c_ref, lambda s: craw.at[s])

    scr = s_ref[...].astype(F32)
    scr = jnp.concatenate([scr, jnp.zeros((LANES - mb, nb), F32)], axis=0)
    wide = -(-nb // LANES) * LANES
    if wide > nb:
        scr = jnp.concatenate([scr, jnp.zeros((LANES, wide - nb), F32)], axis=1)
    scr = scr.T
    for i in range(nr):
        st[i] = jnp.concatenate(
            [scr[i * nk:(i + 1) * nk], jnp.zeros((slot - nk, LANES), F32)], axis=0).astype(BF16)
    row_start(2, lambda s: st.at[s], lambda s: sall.at[s])
    sall[r] = st[r]
    vall[r, pl.ds(0, mb)] = v_ref[...]
    if mb < LANES:
        for i in range(nr):
            vall[i, pl.ds(mb, LANES - mb)] = jnp.zeros((LANES - mb, nv), BF16)
    place(own, j)
    evb[...] = jnp.broadcast_to(ev_ref[...], (LANES, nv)).T
    ec = ec_ref[:, pl.ds(pl.multiple_of(r * cw, cw), cw)]
    low = lax.broadcasted_iota(jnp.int32, (half, LANES), 1) < vj

    def swap(block):
        return pltpu.roll(block, vj, 1)

    def screen(w):
        allv = vall[...].reshape(nr * LANES, nv)
        inner = dot_nt(w, allv)
        tile = jnp.concatenate(
            [(sall[i].astype(F32) * inner[:, i * LANES:(i + 1) * LANES]).astype(BF16)
             for i in range(nr)], axis=1)
        return jnp.dot(tile, allv, preferred_element_type=F32)

    def pack(y, send):
        for p in range(nj // 2):
            top = y[:half, p * LANES:(p + 1) * LANES]
            bottom = y[half:, p * LANES:(p + 1) * LANES]
            send[2 * p] = jnp.where(low, top, swap(bottom)).astype(BF16)
            send[2 * p + 1] = jnp.where(low, swap(top), bottom).astype(BF16)

    def spread(y, send, yall, phase_col, phase_row):
        pack(y, send)
        col_start(phase_col, lambda s: send.at[s], lambda s: yall.at[r, s])
        yall[r, j] = send[j]
        col_wait(phase_col, lambda s: yall.at[r, s])
        row_start(phase_row, lambda s: yall.at[r], lambda s: yall.at[s])

    def term(yall):
        whole = yall[...].reshape(nr * nj * half, LANES)
        lo = clo[...].reshape(nr * nj * half, cw)
        hi = chi[...].reshape(nr * nj * half, cw)
        return dot_tn(whole, lo)[:vj] + dot_tn(whole, hi)[vj:]

    row_wait(0, lambda s: arecv.at[s])
    total = arecv[0].astype(F32)
    for i in range(1, nr):
        total = total + arecv[i].astype(F32)
    w0 = total.astype(BF16)
    row_wait(2, lambda s: sall.at[s])
    row_wait(1, lambda s: vall.at[s, pl.ds(0, mb)])
    spread(screen(w0), ysend0, yall0, 1, 3)
    col_wait(0, lambda s: craw.at[s])
    for s in col_peers:
        place(padded(craw.at[s]), s)
    row_wait(3, lambda s: yall0.at[s])
    k0 = term(yall0)
    mine = pl.ds(pl.multiple_of(j * vj, vj), vj)
    x1 = (ec - evb[mine, :]) * x_ref[0, mine, :] + k0
    x1b = x1.astype(BF16)
    none = jnp.zeros((LANES - vj, cw), BF16)
    lo = clo[...].reshape(nr * nj * half, cw)
    hi = chi[...].reshape(nr * nj * half, cw)
    partial = (dot_nt(lo, jnp.concatenate([x1b, none], axis=0))
               + dot_nt(hi, jnp.concatenate([none, x1b], axis=0)))
    esend[...] = partial.astype(BF16).reshape(esend.shape)
    row_start(4, lambda s: esend.at[s], lambda s: erecv.at[s])
    erecv[r] = esend[r]
    kz0[j] = k0.astype(BF16)
    row_wait(4, lambda s: erecv.at[s])

    total = erecv[0].astype(F32)
    for i in range(1, nr):
        total = total + erecv[i].astype(F32)
    zsend[...] = total.astype(BF16)
    col_start(2, lambda s: zsend.at[s], lambda s: zrecv.at[s])
    col_start(4, lambda s: kz0.at[j], lambda s: kz0.at[s])
    zrecv[j] = zsend[j]
    col_wait(2, lambda s: zrecv.at[s])
    tops, bottoms = [], []
    for p in range(nj // 2):
        a = zrecv[2 * p].astype(F32)
        b = zrecv[2 * p + 1].astype(F32)
        tops.append(jnp.where(low, a, swap(b)))
        bottoms.append(jnp.where(low, swap(a), b))
    w1 = jnp.concatenate(
        [jnp.concatenate(tops, axis=1), jnp.concatenate(bottoms, axis=1)], axis=0).astype(BF16)
    spread(screen(w1), ysend1, yall1, 3, 5)
    col_wait(4, lambda s: kz0.at[s])
    energy = ec - evb[...]
    base = energy * (energy * x_ref[0] + kz0[...].reshape(nv, cw).astype(F32))
    row_wait(5, lambda s: yall1.at[s])
    kz1[j] = term(yall1).astype(BF16)
    col_start(5, lambda s: kz1.at[j], lambda s: kz1.at[s])
    col_wait(5, lambda s: kz1.at[s])
    out_ref[0] = base + kz1[...].reshape(nv, cw).astype(F32)
    for copy in pending:
        copy.wait_send()


def fused(nr, nj, trial, screened, val_points, cond_points, eps_val, eps_cond):
    mb, nv = val_points.shape
    nb, cw = cond_points.shape
    slot = 2 * ROWS16
    half = ROWS16
    scratch = [
        pltpu.VMEM((nr, LANES, nv), BF16),
        pltpu.VMEM((nr, slot, LANES), BF16),
        pltpu.VMEM((nr, slot, LANES), BF16),
        pltpu.VMEM((nr, slot, nv), BF16),
        pltpu.VMEM((nr, slot, nv), BF16),
        pltpu.VMEM((nj, nb, cw), BF16),
        pltpu.VMEM((nr, nj, half, cw), BF16),
        pltpu.VMEM((nr, nj, half, cw), BF16),
        pltpu.VMEM((nv, LANES), F32),
        pltpu.VMEM((nj, half, LANES), BF16),
        pltpu.VMEM((nj, half, LANES), BF16),
        pltpu.VMEM((nr, nj, half, LANES), BF16),
        pltpu.VMEM((nr, nj, half, LANES), BF16),
        pltpu.VMEM((nr, nj, half, LANES), BF16),
        pltpu.VMEM((nr, nj, half, LANES), BF16),
        pltpu.VMEM((nj, half, LANES), BF16),
        pltpu.VMEM((nj, half, LANES), BF16),
        pltpu.VMEM((nj, nv // nj, cw), BF16),
        pltpu.VMEM((nj, nv // nj, cw), BF16),
        pltpu.SemaphoreType.DMA((6, nr)),
        pltpu.SemaphoreType.DMA((6, nr)),
        pltpu.SemaphoreType.DMA((6, nj)),
        pltpu.SemaphoreType.DMA((6, nj)),
    ]
    return pl.pallas_call(
        functools.partial(kernel, nr, nj),
        out_shape=jax.ShapeDtypeStruct(trial.shape, F32),
        in_specs=[pl.BlockSpec(memory_space=pltpu.VMEM)] * 6,
        out_specs=pl.BlockSpec(memory_space=pltpu.VMEM),
        scratch_shapes=scratch,
        compiler_params=pltpu.CompilerParams(
            collective_id=0, has_side_effects=True, vmem_limit_bytes=24 * 2**20),
    )(trial, screened, val_points, cond_points, eps_val[None], eps_cond[None])


def fits(nr, nj, trial, val_points, cond_points):
    mb, nv = val_points.shape
    nb, cw = cond_points.shape
    nk = nb // nr
    return (trial.shape[0] == 1 and cw == LANES and nb % nr == 0 and nk % 8 == 0
            and nk <= 2 * ROWS16 and mb % ROWS16 == 0 and mb <= LANES
            and nj % 2 == 0 and nv % nj == 0 and 2 * (nv // nj) == LANES)


def general(trial, screened, val_points, cond_points, eps_val, eps_cond):
    cond_full = lax.all_gather(cond_points, "row", axis=1, tiled=True)
    energy_full = eps_cond[None, :] - eps_val[:, None]
    width = trial.shape[2]
    offset = lax.axis_index("row") * width
    x_full = lax.all_gather(trial.astype(BF16), "row", axis=2, tiled=True).astype(trial.dtype)
    xb_full = x_full.astype(BF16)
    x_mine = trial
    for step in range(APPLY):
        pair = jnp.einsum(
            "mv,bvc->bmc", val_points, xb_full, preferred_element_type=F32).astype(BF16)
        inner = jnp.einsum("bmc,nc->bmn", pair, cond_full, preferred_element_type=F32)
        tile = (screened[None] * inner).astype(BF16)
        back = jnp.einsum("bmn,nc->bmc", tile, cond_full, preferred_element_type=F32).astype(BF16)
        part_low = jnp.einsum(
            "mv,bmc->bvc", val_points, back, preferred_element_type=F32).astype(BF16)
        partial_terms = lax.optimization_barrier(part_low).astype(F32)
        kernel_full = lax.psum(partial_terms, ("row", "col"))
        x_full = energy_full[None] * x_full + kernel_full
        xb_full = x_full.astype(BF16)
        x_mine = lax.dynamic_slice_in_dim(x_full, offset, width, 2)
    return x_mine


def solution(mesh):
    nr, nj = mesh.shape["row"], mesh.shape["col"]

    def body(trial, screened, val_points, cond_points, eps_val, eps_cond):
        args = (trial, screened, val_points, cond_points, eps_val, eps_cond)
        if fits(nr, nj, trial, val_points, cond_points):
            return fused(nr, nj, *args)
        return general(*args)

    in_specs = (P(None, None, "row"), P("row", "col"), P("row", None), P("col", "row"), P(), P())
    out_specs = P(None, None, "row")
    return jax.shard_map(body, mesh=mesh, in_specs=in_specs, out_specs=out_specs, check_vma=False)
```

```python
import functools

import jax
import jax.numpy as jnp
from jax import lax
from jax.experimental import pallas as pl
from jax.experimental.pallas import tpu as pltpu
from jax.sharding import PartitionSpec as P

APPLY = 2
LANES = 128
ROWS16 = 16
F32 = jnp.float32
BF16 = jnp.bfloat16
MESH = pl.DeviceIdType.MESH


def dot_nt(a, b):
    return lax.dot_general(a, b, (((1,), (1,)), ((), ())), preferred_element_type=F32)


def dot_tn(a, b):
    return lax.dot_general(a, b, (((0,), (0,)), ((), ())), preferred_element_type=F32)


def kernel(nr, nj, x_hbm, s_hbm, v_hbm, c_hbm, ev_hbm, ec_hbm, out_ref,
           xv, sv, cv, evv, ecv, vall, st, sall, asend, arecv, call, evb,
           ysend0, ysend1, yall0, yall1, esend, erecv, kz0,
           local_sem, row_send, row_recv, own_send, own_recv,
           col_send, col_recv, peer_send, peer_recv, mate_send, mate_recv):
    r = lax.axis_index("row")
    j = lax.axis_index("col")
    group, plane = j // 2, lax.rem(j, 2)
    me = r * 2 + plane
    np = nr * 2
    nq = np // nj
    mb, nv = v_hbm.shape
    _, nk, cw = c_hbm.shape
    nb = nq * nk
    vh = nv // 2

    loads = {}
    for i, (name, src, dst) in enumerate([
            ("c", c_hbm, cv), ("x", x_hbm, xv), ("s", s_hbm, sv),
            ("v", v_hbm, vall.at[r, pl.ds(0, mb)]), ("ev", ev_hbm, evv), ("ec", ec_hbm, ecv),
            ("call", c_hbm, call.at[:, j])]):
        loads[name] = pltpu.make_async_copy(src, dst, local_sem.at[i])
        loads[name].start()

    barrier = pltpu.get_barrier_semaphore()
    peers = [lax.rem(me + k, np) for k in range(1, np)]
    row_peers = [lax.rem(r + k, nr) for k in range(1, nr)]
    col_peers = [lax.rem(j + k, nj) for k in range(1, nj)]
    far_groups = [lax.rem(group + k, nj // 2) for k in range(1, nj // 2)]
    for p in peers:
        pl.semaphore_signal(barrier, inc=1, device_id=(p // 2, group * 2 + lax.rem(p, 2)),
                            device_id_type=MESH)
    for g in far_groups:
        for s in range(nr):
            pl.semaphore_signal(barrier, inc=1, device_id=(s, g * 2 + plane),
                                device_id_type=MESH)
        pl.semaphore_signal(barrier, inc=1, device_id=(r, g * 2 + 1 - plane),
                            device_id_type=MESH)
    greeted = np - 1 + (nj // 2 - 1) * (nr + 1)

    pending = []

    def send(copy):
        copy.start()
        pending.append(copy)

    def row_copy(src, dst, peer, slot_id):
        return pltpu.make_async_remote_copy(
            src_ref=src, dst_ref=dst, send_sem=row_send.at[peer],
            recv_sem=row_recv.at[slot_id], device_id=(peer, j), device_id_type=MESH)

    def col_copy(src, dst, peer, slot_id):
        return pltpu.make_async_remote_copy(
            src_ref=src, dst_ref=dst, send_sem=col_send.at[peer],
            recv_sem=col_recv.at[slot_id], device_id=(r, peer), device_id_type=MESH)

    def peer_copy(phase, src, dst, peer, slot_id):
        return pltpu.make_async_remote_copy(
            src_ref=src, dst_ref=dst, send_sem=peer_send.at[phase, peer],
            recv_sem=peer_recv.at[phase, slot_id],
            device_id=(peer // 2, group * 2 + lax.rem(peer, 2)), device_id_type=MESH)

    def owner_copy(phase, src, dst, q, g):
        return pltpu.make_async_remote_copy(
            src_ref=src, dst_ref=dst, send_sem=own_send.at[phase, q, g],
            recv_sem=own_recv.at[phase, r],
            device_id=(q * (nj // 2) + group, g * 2 + plane), device_id_type=MESH)

    def is_self(q, g):
        return jnp.logical_and(q * (nj // 2) + group == r, group == g)

    def owner_send(phase, buffer, target):
        for g in range(nj // 2):
            for q in range(nq):
                @pl.when(jnp.logical_not(is_self(q, g)))
                def _():
                    owner_copy(phase, buffer.at[q], target.at[r], q, g).start()

                @pl.when(is_self(q, g))
                def _():
                    target[r] = buffer[q]

    def owner_wait_send(phase, buffer, target):
        for g in range(nj // 2):
            for q in range(nq):
                @pl.when(jnp.logical_not(is_self(q, g)))
                def _():
                    owner_copy(phase, buffer.at[q], target.at[r], q, g).wait_send()

    holder = lax.rem(r, nj // 2) * 2 + plane

    def owner_wait(phase, target):
        for k in range(nr):
            s = lax.rem(r + k, nr)

            def wait():
                pltpu.make_async_remote_copy(
                    src_ref=target.at[s], dst_ref=target.at[s], send_sem=own_send.at[phase, 0, 0],
                    recv_sem=own_recv.at[phase, s], device_id=(s, holder),
                    device_id_type=MESH).wait_recv()

            if k == 0:
                pl.when(holder != j)(wait)
            else:
                wait()

    def all_send(phase, src_of, dst):
        for p in peers:
            send(peer_copy(phase, src_of(p), dst, p, me))

    def all_wait(phase, dst_of):
        for p in reversed(peers):
            peer_copy(phase, dst_of(p), dst_of(p), p, p).wait_recv()

    loads["c"].wait()
    loads["x"].wait()
    first = dot_nt(cv[...].reshape(nb, cw), xv[0].astype(BF16))
    asend[...] = first.astype(BF16).reshape(asend.shape)

    pl.semaphore_wait(barrier, greeted)
    owner_send(0, asend, arecv)
    for s in row_peers:
        send(row_copy(v_hbm, vall.at[r, pl.ds(0, mb)], s, r))

    loads["s"].wait()
    scr = sv[...].astype(F32)
    scr = jnp.concatenate([scr, jnp.zeros((LANES - mb, nb), F32)], axis=0)
    wide = -(-nb // LANES) * LANES
    if wide > nb:
        scr = jnp.concatenate([scr, jnp.zeros((LANES, wide - nb), F32)], axis=1)
    scr = scr.T
    st[...] = scr[:nb].astype(BF16).reshape(st.shape)
    owner_send(1, st, sall)
    for s in col_peers:
        send(col_copy(c_hbm, call.at[:, j], s, j))

    if mb < LANES:
        for i in range(nr):
            vall[i, pl.ds(mb, LANES - mb)] = jnp.zeros((LANES - mb, nv), BF16)
    for name in ("ev", "ec", "v", "call"):
        loads[name].wait()
    evb[...] = jnp.broadcast_to(evv[...], (LANES, nv)).T
    ec = ecv[:, pl.ds(pl.multiple_of(r * cw, cw), cw)]

    def screen(w):
        allv = vall[...].reshape(nr * LANES, nv)
        inner = dot_nt(w, allv)
        tile = jnp.concatenate(
            [(sall[i].astype(F32) * inner[:, i * LANES:(i + 1) * LANES]).astype(BF16)
             for i in range(nr)], axis=1)
        return jnp.dot(tile, allv, preferred_element_type=F32).astype(BF16)

    owner_wait(0, arecv)
    total = arecv[0].astype(F32)
    for i in range(1, nr):
        total = total + arecv[i].astype(F32)
    w0 = total.astype(BF16)
    for s in reversed(row_peers):
        block = vall.at[s, pl.ds(0, mb)]
        row_copy(block, block, s, s).wait_recv()
    owner_wait(1, sall)
    y0 = screen(w0)
    ysend0[0] = y0[:, :vh]
    ysend0[1] = y0[:, vh:]
    all_send(0, lambda p: ysend0.at[lax.rem(p, 2)], yall0.at[me])
    yall0[me] = ysend0[plane]
    for s in col_peers:
        block = call.at[:, s]
        col_copy(block, block, s, s).wait_recv()
    all_wait(0, lambda p: yall0.at[p])
    cond = call[...].reshape(np * nk, cw)
    k0 = dot_tn(yall0[...].reshape(np * nk, vh), cond)
    mine = pl.ds(pl.multiple_of(plane * vh, vh), vh)
    x1 = (ec - evb[mine, :]) * xv[0, mine, :] + k0
    esend[...] = dot_nt(cond, x1.astype(BF16)).astype(BF16).reshape(esend.shape)
    all_send(1, lambda p: esend.at[p], erecv.at[plane, r])
    erecv[plane, r] = esend[me]
    kz0[plane] = k0.astype(BF16)

    def mate_copy(which):
        return pltpu.make_async_remote_copy(
            src_ref=kz0.at[which], dst_ref=kz0.at[which], send_sem=mate_send.at[0],
            recv_sem=mate_recv.at[0], device_id=(r, group * 2 + 1 - plane), device_id_type=MESH)

    send(mate_copy(plane))
    all_wait(1, lambda p: erecv.at[lax.rem(p, 2), p // 2])

    halves = []
    for h in range(2):
        total = erecv[h, 0].astype(F32)
        for i in range(1, nr):
            total = total + erecv[h, i].astype(F32)
        halves.append(total)
    y1 = screen(jnp.concatenate(halves, axis=1).astype(BF16))
    ysend1[...] = y1
    all_send(2, lambda p: ysend1, yall1.at[me])
    yall1[me] = ysend1[...]
    mate_copy(1 - plane).wait_recv()
    energy = ec - evb[...]
    base = energy * (energy * xv[0] + kz0[...].reshape(nv, cw).astype(F32))
    all_wait(2, lambda p: yall1.at[p])
    out_ref[0] = base + dot_tn(yall1[...].reshape(np * nk, nv), cond)
    for copy in pending:
        copy.wait_send()
    owner_wait_send(0, asend, arecv)
    owner_wait_send(1, st, sall)


def fused(nr, nj, trial, screened, val_points, cond_points, eps_val, eps_cond):
    mb, nv = val_points.shape
    nb, cw = cond_points.shape
    np = 2 * nr
    nq = np // nj
    nk = nb // nq
    vh = nv // 2
    ng = nj // 2
    scratch = [
        pltpu.VMEM(trial.shape, F32),
        pltpu.VMEM(screened.shape, BF16),
        pltpu.VMEM((nq, nk, cw), BF16),
        pltpu.VMEM((1, nv), F32),
        pltpu.VMEM((1, eps_cond.shape[0]), F32),
        pltpu.VMEM((nr, LANES, nv), BF16),
        pltpu.VMEM((nq, nk, LANES), BF16),
        pltpu.VMEM((nr, nk, LANES), BF16),
        pltpu.VMEM((nq, nk, nv), BF16),
        pltpu.VMEM((nr, nk, nv), BF16),
        pltpu.VMEM((nq, nj, nk, cw), BF16),
        pltpu.VMEM((nv, LANES), F32),
        pltpu.VMEM((2, nk, vh), BF16),
        pltpu.VMEM((nk, nv), BF16),
        pltpu.VMEM((np, nk, vh), BF16),
        pltpu.VMEM((np, nk, nv), BF16),
        pltpu.VMEM((np, nk, vh), BF16),
        pltpu.VMEM((2, nr, nk, vh), BF16),
        pltpu.VMEM((2, vh, cw), BF16),
        pltpu.SemaphoreType.DMA((7,)),
        pltpu.SemaphoreType.DMA((nr,)),
        pltpu.SemaphoreType.DMA((nr,)),
        pltpu.SemaphoreType.DMA((2, nq, ng)),
        pltpu.SemaphoreType.DMA((2, nr)),
        pltpu.SemaphoreType.DMA((nj,)),
        pltpu.SemaphoreType.DMA((nj,)),
        pltpu.SemaphoreType.DMA((3, np)),
        pltpu.SemaphoreType.DMA((3, np)),
        pltpu.SemaphoreType.DMA((1,)),
        pltpu.SemaphoreType.DMA((1,)),
    ]
    return pl.pallas_call(
        functools.partial(kernel, nr, nj),
        out_shape=jax.ShapeDtypeStruct(trial.shape, F32),
        in_specs=[pl.BlockSpec(memory_space=pl.ANY)] * 6,
        out_specs=pl.BlockSpec(memory_space=pltpu.VMEM),
        scratch_shapes=scratch,
        compiler_params=pltpu.CompilerParams(
            collective_id=0, has_side_effects=True, vmem_limit_bytes=48 * 2**20),
    )(trial, screened, val_points, cond_points.reshape(nq, nk, cw), eps_val[None], eps_cond[None])


def fits(nr, nj, trial, val_points, cond_points):
    mb, nv = val_points.shape
    nb, cw = cond_points.shape
    if nj % 2 or (2 * nr) % nj or nb % (2 * nr // nj):
        return False
    nk = nb // (2 * nr // nj)
    return (trial.shape[0] == 1 and cw == LANES and nk % ROWS16 == 0
            and mb % ROWS16 == 0 and mb <= LANES and nv == 2 * LANES)


def general(trial, screened, val_points, cond_points, eps_val, eps_cond):
    cond_full = lax.all_gather(cond_points, "row", axis=1, tiled=True)
    energy_full = eps_cond[None, :] - eps_val[:, None]
    width = trial.shape[2]
    offset = lax.axis_index("row") * width
    x_full = lax.all_gather(trial.astype(BF16), "row", axis=2, tiled=True).astype(trial.dtype)
    xb_full = x_full.astype(BF16)
    x_mine = trial
    for step in range(APPLY):
        pair = jnp.einsum(
            "mv,bvc->bmc", val_points, xb_full, preferred_element_type=F32).astype(BF16)
        inner = jnp.einsum("bmc,nc->bmn", pair, cond_full, preferred_element_type=F32)
        tile = (screened[None] * inner).astype(BF16)
        back = jnp.einsum("bmn,nc->bmc", tile, cond_full, preferred_element_type=F32).astype(BF16)
        part_low = jnp.einsum(
            "mv,bmc->bvc", val_points, back, preferred_element_type=F32).astype(BF16)
        partial_terms = lax.optimization_barrier(part_low).astype(F32)
        kernel_full = lax.psum(partial_terms, ("row", "col"))
        x_full = energy_full[None] * x_full + kernel_full
        xb_full = x_full.astype(BF16)
        x_mine = lax.dynamic_slice_in_dim(x_full, offset, width, 2)
    return x_mine


def solution(mesh):
    nr, nj = mesh.shape["row"], mesh.shape["col"]

    def body(trial, screened, val_points, cond_points, eps_val, eps_cond):
        args = (trial, screened, val_points, cond_points, eps_val, eps_cond)
        if fits(nr, nj, trial, val_points, cond_points):
            return fused(nr, nj, *args)
        return general(*args)

    in_specs = (P(None, None, "row"), P("row", "col"), P("row", None), P("col", "row"), P(), P())
    out_specs = P(None, None, "row")
    return jax.shard_map(body, mesh=mesh, in_specs=in_specs, out_specs=out_specs, check_vma=False)
```

```python
import functools

import jax
import jax.numpy as jnp
from jax import lax
from jax.experimental import pallas as pl
from jax.experimental.pallas import tpu as pltpu
from jax.sharding import PartitionSpec as P

APPLY = 2
LANES = 128
ROWS16 = 16
F32 = jnp.float32
BF16 = jnp.bfloat16
MESH = pl.DeviceIdType.MESH


def dot_nt(a, b):
    return lax.dot_general(a, b, (((1,), (1,)), ((), ())), preferred_element_type=F32)


def kernel(nr, nj, x_hbm, s_hbm, v_hbm, c_hbm, ev_hbm, ec_hbm, out_ref,
           xv, sv, cv, evv, ecv, vall, st, sall, asend, arecv, call, evb,
           ysend0, ysend1, yall0, yall1, esend, erecv, kz0, w0, b1t, condt,
           local_sem, row_send, row_recv, own_send, own_recv,
           col_send, col_recv, peer_send, peer_recv, mate_send, mate_recv, far_send, far_recv):
    r = lax.axis_index("row")
    j = lax.axis_index("col")
    group, plane = j // 2, lax.rem(j, 2)
    me = r * 2 + plane
    np = nr * 2
    nq = np // nj
    mb, nv = v_hbm.shape
    _, nk, cw = c_hbm.shape
    nb = nq * nk
    vh = nv // 2

    loads = {}
    for i, (name, src, dst) in enumerate([
            ("c", c_hbm, cv), ("x", x_hbm, xv), ("s", s_hbm, sv),
            ("v", v_hbm, vall.at[r, pl.ds(0, mb)]), ("ev", ev_hbm, evv), ("ec", ec_hbm, ecv),
            ("call", c_hbm, call.at[:, j])]):
        loads[name] = pltpu.make_async_copy(src, dst, local_sem.at[i])
        loads[name].start()

    barrier = pltpu.get_barrier_semaphore()
    steps = sorted(range(1, np), key=lambda k: abs(k - np // 2))
    peers = [lax.rem(me + k, np) for k in steps]
    sources = [lax.rem(me + np - k, np) for k in steps]
    row_peers = [lax.rem(r + k, nr) for k in range(1, nr)]
    col_peers = [lax.rem(j + k, nj) for k in range(1, nj)]
    far_groups = [lax.rem(group + k, nj // 2) for k in range(1, nj // 2)]
    for p in peers:
        pl.semaphore_signal(barrier, inc=1, device_id=(p // 2, group * 2 + lax.rem(p, 2)),
                            device_id_type=MESH)
    for g in far_groups:
        for s in range(nr):
            pl.semaphore_signal(barrier, inc=1, device_id=(s, g * 2 + plane),
                                device_id_type=MESH)
        pl.semaphore_signal(barrier, inc=1, device_id=(r, g * 2 + 1 - plane),
                            device_id_type=MESH)
    greeted = np - 1 + (nj // 2 - 1) * (nr + 1)

    pending = []

    def send(copy):
        copy.start()
        pending.append(copy)

    def row_copy(src, dst, peer, slot_id):
        return pltpu.make_async_remote_copy(
            src_ref=src, dst_ref=dst, send_sem=row_send.at[peer],
            recv_sem=row_recv.at[slot_id], device_id=(peer, j), device_id_type=MESH)

    def col_copy(src, dst, peer, slot_id):
        return pltpu.make_async_remote_copy(
            src_ref=src, dst_ref=dst, send_sem=col_send.at[peer],
            recv_sem=col_recv.at[slot_id], device_id=(r, peer), device_id_type=MESH)

    def peer_copy(phase, src, dst, peer, slot_id):
        return pltpu.make_async_remote_copy(
            src_ref=src, dst_ref=dst, send_sem=peer_send.at[phase, peer],
            recv_sem=peer_recv.at[phase, slot_id],
            device_id=(peer // 2, group * 2 + lax.rem(peer, 2)), device_id_type=MESH)

    def owner_copy(phase, src, dst, q, g):
        return pltpu.make_async_remote_copy(
            src_ref=src, dst_ref=dst, send_sem=own_send.at[phase, q, g],
            recv_sem=own_recv.at[phase, r],
            device_id=(q * (nj // 2) + group, g * 2 + plane), device_id_type=MESH)

    def is_self(q, g):
        return jnp.logical_and(q * (nj // 2) + group == r, group == g)

    groups = [lax.rem(group + k, nj // 2) for k in range(nj // 2)]

    def owner_each(q, g, away, here):
        if g is groups[0]:
            itself = q * (nj // 2) + group == r
            pl.when(jnp.logical_not(itself))(away)
            if here is not None:
                pl.when(itself)(here)
        else:
            away()

    def owner_send(phase, buffer, target, chosen):
        for g in chosen:
            for q in range(nq):
                def away():
                    owner_copy(phase, buffer.at[q], target.at[r], q, g).start()

                def here():
                    target[r] = buffer[q]

                owner_each(q, g, away, here)

    def owner_wait_send(phase, buffer, target, chosen):
        for g in chosen:
            for q in range(nq):
                def away():
                    owner_copy(phase, buffer.at[q], target.at[r], q, g).wait_send()

                owner_each(q, g, away, None)

    holder = lax.rem(r, nj // 2) * 2 + plane
    holds = holder == j

    def owner_wait(phase, target, s):
        pltpu.make_async_remote_copy(
            src_ref=target.at[s], dst_ref=target.at[s], send_sem=own_send.at[phase, 0, 0],
            recv_sem=own_recv.at[phase, s], device_id=(s, holder),
            device_id_type=MESH).wait_recv()

    def far_copy(g):
        return pltpu.make_async_remote_copy(
            src_ref=w0, dst_ref=w0, send_sem=far_send.at[g], recv_sem=far_recv.at[0],
            device_id=(r, g * 2 + plane), device_id_type=MESH)

    def all_send(phase, src_of, dst):
        for p in peers:
            send(peer_copy(phase, src_of(p), dst, p, me))

    def all_wait(phase, dst_of):
        for p in sources:
            peer_copy(phase, dst_of(p), dst_of(p), p, p).wait_recv()

    loads["c"].wait()
    loads["x"].wait()
    first = dot_nt(cv[...].reshape(nb, cw), xv[0].astype(BF16))
    asend[...] = first.astype(BF16).reshape(asend.shape)

    loads["s"].wait()
    scr = sv[...].astype(F32)
    scr = jnp.concatenate([scr, jnp.zeros((LANES - mb, nb), F32)], axis=0)
    wide = -(-nb // LANES) * LANES
    if wide > nb:
        scr = jnp.concatenate([scr, jnp.zeros((LANES, wide - nb), F32)], axis=1)
    scr = scr.T
    st[...] = scr[:nb].astype(BF16).reshape(st.shape)

    pl.semaphore_wait(barrier, greeted)
    owner_send(0, asend, arecv, groups[:1])
    owner_send(1, st, sall, groups[1:])
    for s in row_peers:
        send(row_copy(v_hbm, vall.at[r, pl.ds(0, mb)], s, r))
    owner_send(1, st, sall, groups[:1])
    for s in col_peers:
        send(col_copy(c_hbm, call.at[:, j], s, j))

    if mb < LANES:
        for i in range(nr):
            vall[i, pl.ds(mb, LANES - mb)] = jnp.zeros((LANES - mb, nv), BF16)
    for name in ("ev", "ec", "v", "call"):
        loads[name].wait()
    evb[...] = jnp.broadcast_to(evv[...], (LANES, nv)).T
    ec = ecv[:, pl.ds(pl.multiple_of(r * cw, cw), cw)]

    def screen(w):
        allv = vall[...].reshape(nr * LANES, nv)
        inner = dot_nt(w, allv)
        tile = jnp.concatenate(
            [(sall[i].astype(F32) * inner[:, i * LANES:(i + 1) * LANES]).astype(BF16)
             for i in range(nr)], axis=1)
        return jnp.dot(tile, allv, preferred_element_type=F32).astype(BF16)

    mine = pl.ds(pl.multiple_of(plane * vh, vh), vh)
    b1t[...] = ((ec - evb[mine, :]) * xv[0, mine, :]).T

    @pl.when(holds)
    def _():
        for k in range(1, nr):
            owner_wait(0, arecv, lax.rem(r + k, nr))
        total = arecv[0].astype(F32)
        for i in range(1, nr):
            total = total + arecv[i].astype(F32)
        w0[...] = total.astype(BF16)
        for g in groups[1:]:
            far_copy(g).start()

    for s in reversed(row_peers):
        block = vall.at[s, pl.ds(0, mb)]
        row_copy(block, block, s, s).wait_recv()
    for k in range(1, nr):
        owner_wait(1, sall, lax.rem(r + k, nr))

    @pl.when(jnp.logical_not(holds))
    def _():
        owner_wait(1, sall, r)
        far_copy(group).wait_recv()

    y0 = screen(w0[...])
    ysend0[0] = y0[:, :vh]
    ysend0[1] = y0[:, vh:]
    all_send(0, lambda p: ysend0.at[lax.rem(p, 2)], yall0.at[me])
    yall0[me] = ysend0[plane]
    for s in col_peers:
        block = call.at[:, s]
        col_copy(block, block, s, s).wait_recv()
    condt[...] = call[...].reshape(np * nk, cw).T
    all_wait(0, lambda p: yall0.at[p])
    k0t = jnp.dot(condt[...], yall0[...].reshape(np * nk, vh), preferred_element_type=F32)
    x1t = (b1t[...] + k0t).astype(BF16)

    def kernel_block(p):
        cond = call[p // nj, lax.rem(p, nj)]
        esend[p] = jnp.dot(cond, x1t, preferred_element_type=F32).astype(BF16)

    for p in peers:
        kernel_block(p)
        send(peer_copy(1, esend.at[p], erecv.at[plane, r], p, me))
    kernel_block(me)
    erecv[plane, r] = esend[me]
    kz0[plane] = k0t.astype(BF16)

    def mate_copy(which):
        return pltpu.make_async_remote_copy(
            src_ref=kz0.at[which], dst_ref=kz0.at[which], send_sem=mate_send.at[0],
            recv_sem=mate_recv.at[0], device_id=(r, group * 2 + 1 - plane), device_id_type=MESH)

    send(mate_copy(plane))
    all_wait(1, lambda p: erecv.at[lax.rem(p, 2), p // 2])

    halves = []
    for h in range(2):
        total = erecv[h, 0].astype(F32)
        for i in range(1, nr):
            total = total + erecv[h, i].astype(F32)
        halves.append(total)
    ysend1[...] = screen(jnp.concatenate(halves, axis=1).astype(BF16))
    all_send(2, lambda p: ysend1, yall1.at[me])
    yall1[me] = ysend1[...]
    mate_copy(1 - plane).wait_recv()
    energy = ec - evb[...]
    k0 = jnp.concatenate([kz0[h].astype(F32).T for h in range(2)], axis=0)
    out_ref[0] = energy * (energy * xv[0] + k0)
    all_wait(2, lambda p: yall1.at[p])
    k1t = jnp.dot(condt[...], yall1[...].reshape(np * nk, nv), preferred_element_type=F32)
    out_ref[0] += k1t.T
    for copy in pending:
        copy.wait_send()
    owner_wait_send(0, asend, arecv, groups[:1])
    owner_wait_send(1, st, sall, groups)

    @pl.when(holds)
    def _():
        for g in groups[1:]:
            far_copy(g).wait_send()


def fused(nr, nj, trial, screened, val_points, cond_points, eps_val, eps_cond):
    mb, nv = val_points.shape
    nb, cw = cond_points.shape
    np = 2 * nr
    nq = np // nj
    nk = nb // nq
    vh = nv // 2
    ng = nj // 2
    scratch = [
        pltpu.VMEM(trial.shape, F32),
        pltpu.VMEM(screened.shape, BF16),
        pltpu.VMEM((nq, nk, cw), BF16),
        pltpu.VMEM((1, nv), F32),
        pltpu.VMEM((1, eps_cond.shape[0]), F32),
        pltpu.VMEM((nr, LANES, nv), BF16),
        pltpu.VMEM((nq, nk, LANES), BF16),
        pltpu.VMEM((nr, nk, LANES), BF16),
        pltpu.VMEM((nq, nk, nv), BF16),
        pltpu.VMEM((nr, nk, nv), BF16),
        pltpu.VMEM((nq, nj, nk, cw), BF16),
        pltpu.VMEM((nv, LANES), F32),
        pltpu.VMEM((2, nk, vh), BF16),
        pltpu.VMEM((nk, nv), BF16),
        pltpu.VMEM((np, nk, vh), BF16),
        pltpu.VMEM((np, nk, nv), BF16),
        pltpu.VMEM((np, nk, vh), BF16),
        pltpu.VMEM((2, nr, nk, vh), BF16),
        pltpu.VMEM((2, cw, vh), BF16),
        pltpu.VMEM((nk, nv), BF16),
        pltpu.VMEM((cw, vh), F32),
        pltpu.VMEM((cw, np * nk), BF16),
        pltpu.SemaphoreType.DMA((7,)),
        pltpu.SemaphoreType.DMA((nr,)),
        pltpu.SemaphoreType.DMA((nr,)),
        pltpu.SemaphoreType.DMA((2, nq, ng)),
        pltpu.SemaphoreType.DMA((2, nr)),
        pltpu.SemaphoreType.DMA((nj,)),
        pltpu.SemaphoreType.DMA((nj,)),
        pltpu.SemaphoreType.DMA((3, np)),
        pltpu.SemaphoreType.DMA((3, np)),
        pltpu.SemaphoreType.DMA((1,)),
        pltpu.SemaphoreType.DMA((1,)),
        pltpu.SemaphoreType.DMA((ng,)),
        pltpu.SemaphoreType.DMA((1,)),
    ]
    return pl.pallas_call(
        functools.partial(kernel, nr, nj),
        out_shape=jax.ShapeDtypeStruct(trial.shape, F32),
        in_specs=[pl.BlockSpec(memory_space=pltpu.HBM)] * 6,
        out_specs=pl.BlockSpec(memory_space=pltpu.VMEM),
        scratch_shapes=scratch,
        compiler_params=pltpu.CompilerParams(
            collective_id=0, has_side_effects=True, vmem_limit_bytes=64 * 2**20 - 65536),
    )(trial, screened, val_points, cond_points.reshape(nq, nk, cw), eps_val[None], eps_cond[None])


def fits(nr, nj, trial, val_points, cond_points):
    mb, nv = val_points.shape
    nb, cw = cond_points.shape
    if nj % 2 or (2 * nr) % nj or nb % (2 * nr // nj):
        return False
    nk = nb // (2 * nr // nj)
    return (trial.shape[0] == 1 and cw == LANES and nk % ROWS16 == 0
            and mb % ROWS16 == 0 and mb <= LANES and nv == 2 * LANES)


def general(trial, screened, val_points, cond_points, eps_val, eps_cond):
    cond_full = lax.all_gather(cond_points, "row", axis=1, tiled=True)
    energy_full = eps_cond[None, :] - eps_val[:, None]
    width = trial.shape[2]
    offset = lax.axis_index("row") * width
    x_full = lax.all_gather(trial.astype(BF16), "row", axis=2, tiled=True).astype(trial.dtype)
    xb_full = x_full.astype(BF16)
    x_mine = trial
    for step in range(APPLY):
        pair = jnp.einsum(
            "mv,bvc->bmc", val_points, xb_full, preferred_element_type=F32).astype(BF16)
        inner = jnp.einsum("bmc,nc->bmn", pair, cond_full, preferred_element_type=F32)
        tile = (screened[None] * inner).astype(BF16)
        back = jnp.einsum("bmn,nc->bmc", tile, cond_full, preferred_element_type=F32).astype(BF16)
        part_low = jnp.einsum(
            "mv,bmc->bvc", val_points, back, preferred_element_type=F32).astype(BF16)
        partial_terms = lax.optimization_barrier(part_low).astype(F32)
        kernel_full = lax.psum(partial_terms, ("row", "col"))
        x_full = energy_full[None] * x_full + kernel_full
        xb_full = x_full.astype(BF16)
        x_mine = lax.dynamic_slice_in_dim(x_full, offset, width, 2)
    return x_mine


def solution(mesh):
    nr, nj = mesh.shape["row"], mesh.shape["col"]

    def body(trial, screened, val_points, cond_points, eps_val, eps_cond):
        args = (trial, screened, val_points, cond_points, eps_val, eps_cond)
        if fits(nr, nj, trial, val_points, cond_points):
            return fused(nr, nj, *args)
        return general(*args)

    in_specs = (P(None, None, "row"), P("row", "col"), P("row", None), P("col", "row"), P(), P())
    out_specs = P(None, None, "row")
    return jax.shard_map(body, mesh=mesh, in_specs=in_specs, out_specs=out_specs, check_vma=False)
```

```python
import functools

import jax
import jax.numpy as jnp
from jax import lax
from jax.experimental import pallas as pl
from jax.experimental.pallas import tpu as pltpu
from jax.sharding import PartitionSpec as P

APPLY = 2
LANES = 128
ROWS16 = 16
F32 = jnp.float32
BF16 = jnp.bfloat16
MESH = pl.DeviceIdType.MESH


def dot_nt(a, b):
    return lax.dot_general(a, b, (((1,), (1,)), ((), ())), preferred_element_type=F32)


def kernel(nr, nj, x_hbm, s_hbm, v_hbm, c_hbm, ev_hbm, ec_hbm, base_hbm, k1_ref,
           xv, sv, cv, evv, ecv, vall, st, sall, asend, arecv, call, evb,
           ysend0, ysend1, yall0, yall1, esend, erecv, kz0, w0, b1t, condt, basev,
           local_sem, own_send, own_recv, col_send, col_recv, peer_send, peer_recv,
           mate_send, mate_recv, far_send, far_recv,
           val_send, val_recv, pass_send, pass_recv):
    r = lax.axis_index("row")
    j = lax.axis_index("col")
    group, plane = j // 2, lax.rem(j, 2)
    me = r * 2 + plane
    np = nr * 2
    nq = np // nj
    mb, nv = v_hbm.shape
    _, nk, cw = c_hbm.shape
    nb = nq * nk
    vh = nv // 2

    loads = {}

    def load(names):
        for name, src, dst in names:
            loads[name] = pltpu.make_async_copy(src, dst, local_sem.at[len(loads)])
            loads[name].start()

    load([("c", c_hbm, cv), ("x", x_hbm, xv)])
    barrier = pltpu.get_barrier_semaphore()
    steps = sorted(range(1, np), key=lambda k: abs(k - np // 2))
    peers = [lax.rem(me + k, np) for k in steps]
    chips = [lax.rem(r + 2 * k, nr) for k in range(1, nr // 2)]
    mate = r + 1 - 2 * lax.rem(r, 2)
    col_peers = [lax.rem(j + k, nj) for k in range(1, nj)]
    far_groups = [lax.rem(group + k, nj // 2) for k in range(1, nj // 2)]
    for p in peers:
        pl.semaphore_signal(barrier, inc=1, device_id=(p // 2, group * 2 + lax.rem(p, 2)),
                            device_id_type=MESH)
    for g in far_groups:
        for s in range(nr):
            pl.semaphore_signal(barrier, inc=1, device_id=(s, g * 2 + plane),
                                device_id_type=MESH)
        pl.semaphore_signal(barrier, inc=1, device_id=(r, g * 2 + 1 - plane),
                            device_id_type=MESH)
    greeted = np - 1 + (nj // 2 - 1) * (nr + 1)

    load([("v", v_hbm, vall.at[r, pl.ds(0, mb)]), ("s", s_hbm, sv), ("ev", ev_hbm, evv),
          ("ec", ec_hbm, ecv), ("call", c_hbm, call.at[:, j])])

    def remote(src, dst, send_sem, recv_sem, row, col):
        return pltpu.make_async_remote_copy(
            src_ref=src, dst_ref=dst, send_sem=send_sem, recv_sem=recv_sem,
            device_id=(row, col), device_id_type=MESH)

    def arrived(ref, sem):
        remote(ref, ref, col_send.at[0], sem, mate, j).wait_recv()

    def sent(ref, sem):
        remote(ref, ref, sem, col_recv.at[0], mate, j).wait_send()

    def val_block(s):
        return vall.at[s, pl.ds(0, mb)]

    def val_copy(s):
        return remote(v_hbm, val_block(r), val_send.at[s // 2], val_recv.at[r // 2], s, j)

    def pass_copy(s):
        return remote(val_block(s), val_block(s), pass_send.at[0], pass_recv.at[0], mate, j)

    def peer_copy(phase, src, dst, peer):
        return remote(src, dst, peer_send.at[phase], peer_recv.at[phase],
                      peer // 2, group * 2 + lax.rem(peer, 2))

    def owner_copy(phase, src, dst, q, g):
        return remote(src, dst, own_send.at[phase], own_recv.at[phase],
                      q * (nj // 2) + group, g * 2 + plane)

    groups = [lax.rem(group + k, nj // 2) for k in range(nj // 2)]

    def owner_each(q, g, away, here):
        if g is groups[0]:
            itself = q * (nj // 2) + group == r
            pl.when(jnp.logical_not(itself))(away)
            if here is not None:
                pl.when(itself)(here)
        else:
            away()

    def owner_send(phase, buffer, target, chosen):
        for g in chosen:
            for q in range(nq):
                def away():
                    owner_copy(phase, buffer.at[q], target.at[r], q, g).start()

                def here():
                    target[r] = buffer[q]

                owner_each(q, g, away, here)

    holder = lax.rem(r, nj // 2) * 2 + plane
    holds = holder == j

    def far_copy(g):
        return remote(w0, w0, far_send.at[0], far_recv.at[0], r, g * 2 + plane)

    def all_send(phase, src_of, dst):
        for p in peers:
            peer_copy(phase, src_of(p), dst, p).start()

    loads["c"].wait()
    loads["x"].wait()
    first = dot_nt(cv[...].reshape(nb, cw), xv[0].astype(BF16))
    asend[...] = first.astype(BF16).reshape(asend.shape)

    pl.semaphore_wait(barrier, greeted)
    owner_send(0, asend, arecv, groups[:1])
    for s in chips:
        val_copy(s).start()
    loads["v"].wait()
    pass_copy(r).start()

    loads["s"].wait()
    scr = sv[...].astype(F32)
    scr = jnp.concatenate([scr, jnp.zeros((LANES - mb, nb), F32)], axis=0)
    wide = -(-nb // LANES) * LANES
    if wide > nb:
        scr = jnp.concatenate([scr, jnp.zeros((LANES, wide - nb), F32)], axis=1)
    scr = scr.T
    st[...] = scr[:nb].astype(BF16).reshape(st.shape)
    owner_send(1, st, sall, groups[1:] + groups[:1])
    for s in col_peers:
        remote(c_hbm, call.at[:, j], col_send.at[0], col_recv.at[0], r, s).start()

    if mb < LANES:
        for i in range(nr):
            vall[i, pl.ds(mb, LANES - mb)] = jnp.zeros((LANES - mb, nv), BF16)
    for name in ("ev", "ec", "call"):
        loads[name].wait()
    evb[...] = jnp.broadcast_to(evv[...], (LANES, nv)).T
    ec = ecv[:, pl.ds(pl.multiple_of(r * cw, cw), cw)]

    def screen(w):
        allv = vall[...].reshape(nr * LANES, nv)
        inner = dot_nt(w, allv)
        tile = jnp.concatenate(
            [(sall[i].astype(F32) * inner[:, i * LANES:(i + 1) * LANES]).astype(BF16)
             for i in range(nr)], axis=1)
        return jnp.dot(tile, allv, preferred_element_type=F32).astype(BF16)

    mine = pl.ds(pl.multiple_of(plane * vh, vh), vh)
    b1t[...] = ((ec - evb[mine, :]) * xv[0, mine, :]).T

    @pl.when(holds)
    def _():
        arrived(arecv.at[pl.ds(0, nr - 1)], own_recv.at[0])
        total = arecv[0].astype(F32)
        for i in range(1, nr):
            total = total + arecv[i].astype(F32)
        w0[...] = total.astype(BF16)
        for g in groups[1:]:
            far_copy(g).start()

    for s in reversed(chips):
        arrived(val_block(s), val_recv.at[s // 2])
        pass_copy(s).start()

    @pl.when(holds)
    def _():
        arrived(sall.at[pl.ds(0, nr - 1)], own_recv.at[1])

    @pl.when(jnp.logical_not(holds))
    def _():
        arrived(sall, own_recv.at[1])
        arrived(w0, far_recv.at[0])

    arrived(vall.at[pl.ds(0, nr // 2), pl.ds(0, mb)], pass_recv.at[0])
    y0 = screen(w0[...])
    ysend0[0] = y0[:, :vh]
    ysend0[1] = y0[:, vh:]
    all_send(0, lambda p: ysend0.at[lax.rem(p, 2)], yall0.at[me])
    yall0[me] = ysend0[plane]
    arrived(call.at[:, pl.ds(0, nj - 1)], col_recv.at[0])
    condt[...] = call[...].reshape(np * nk, cw).T
    for s in chips:
        val_copy(s).wait_send()
    sent(vall.at[pl.ds(0, nr // 2), pl.ds(0, mb)], pass_send.at[0])
    sent(call.at[:, pl.ds(0, nj - 1)], col_send.at[0])

    @pl.when(holds)
    def _():
        sent(asend.at[pl.ds(0, nq - 1)], own_send.at[0])
        sent(sall.at[pl.ds(0, nr - 1)], own_send.at[1])
        sent(arecv.at[pl.ds(0, nj // 2 - 1)], far_send.at[0])

    @pl.when(jnp.logical_not(holds))
    def _():
        sent(asend, own_send.at[0])
        sent(sall, own_send.at[1])

    arrived(yall0.at[pl.ds(0, np - 1)], peer_recv.at[0])
    k0t = jnp.dot(condt[...], yall0[...].reshape(np * nk, vh), preferred_element_type=F32)
    x1t = (b1t[...] + k0t).astype(BF16)

    def kernel_block(p):
        cond = call[p // nj, lax.rem(p, nj)]
        esend[p] = jnp.dot(cond, x1t, preferred_element_type=F32).astype(BF16)

    for p in peers:
        kernel_block(p)
        peer_copy(1, esend.at[p], erecv.at[plane * nr + r], p).start()
    kernel_block(me)
    erecv[plane * nr + r] = esend[me]
    kz0[plane] = k0t.astype(BF16)

    other = group * 2 + 1 - plane
    swap = remote(kz0.at[plane], kz0.at[plane], mate_send.at[0], mate_recv.at[0], r, other)
    swap.start()
    sent(yall0.at[pl.ds(0, np - 1)], peer_send.at[0])
    arrived(erecv.at[pl.ds(0, np - 1)], peer_recv.at[1])

    halves = []
    for h in range(2):
        total = erecv[h * nr].astype(F32)
        for i in range(1, nr):
            total = total + erecv[h * nr + i].astype(F32)
        halves.append(total)
    ysend1[...] = screen(jnp.concatenate(halves, axis=1).astype(BF16))
    all_send(2, lambda p: ysend1, yall1.at[me])
    yall1[me] = ysend1[...]
    arrived(kz0.at[1 - plane], mate_recv.at[0])
    energy = ec - evb[...]
    k0 = jnp.concatenate([kz0[h].astype(F32).T for h in range(2)], axis=0)
    basev[0] = energy * (energy * xv[0] + k0)
    store = pltpu.make_async_copy(basev, base_hbm, local_sem.at[len(loads)])
    store.start()
    swap.wait_send()
    sent(erecv.at[pl.ds(0, np - 1)], peer_send.at[1])
    arrived(yall1.at[pl.ds(0, np - 1)], peer_recv.at[2])
    k1t = jnp.dot(condt[...], yall1[...].reshape(np * nk, nv), preferred_element_type=F32)
    k1_ref[0] = k1t.T
    store.wait()
    sent(yall1.at[pl.ds(0, np - 1)], peer_send.at[2])


def fused(nr, nj, trial, screened, val_points, cond_points, eps_val, eps_cond):
    mb, nv = val_points.shape
    nb, cw = cond_points.shape
    np = 2 * nr
    nq = np // nj
    nk = nb // nq
    vh = nv // 2
    ng = nj // 2
    scratch = [
        pltpu.VMEM(trial.shape, F32),
        pltpu.VMEM(screened.shape, BF16),
        pltpu.VMEM((nq, nk, cw), BF16),
        pltpu.VMEM((1, nv), F32),
        pltpu.VMEM((1, eps_cond.shape[0]), F32),
        pltpu.VMEM((nr, LANES, nv), BF16),
        pltpu.VMEM((nq, nk, LANES), BF16),
        pltpu.VMEM((nr, nk, LANES), BF16),
        pltpu.VMEM((nq, nk, nv), BF16),
        pltpu.VMEM((nr, nk, nv), BF16),
        pltpu.VMEM((nq, nj, nk, cw), BF16),
        pltpu.VMEM((nv, LANES), F32),
        pltpu.VMEM((2, nk, vh), BF16),
        pltpu.VMEM((nk, nv), BF16),
        pltpu.VMEM((np, nk, vh), BF16),
        pltpu.VMEM((np, nk, nv), BF16),
        pltpu.VMEM((np, nk, vh), BF16),
        pltpu.VMEM((np, nk, vh), BF16),
        pltpu.VMEM((2, cw, vh), BF16),
        pltpu.VMEM((nk, nv), BF16),
        pltpu.VMEM((cw, vh), F32),
        pltpu.VMEM((cw, np * nk), BF16),
        pltpu.VMEM(trial.shape, F32),
        pltpu.SemaphoreType.DMA((8,)),
        pltpu.SemaphoreType.DMA((2,)),
        pltpu.SemaphoreType.DMA((2,)),
        pltpu.SemaphoreType.DMA((1,)),
        pltpu.SemaphoreType.DMA((1,)),
        pltpu.SemaphoreType.DMA((3,)),
        pltpu.SemaphoreType.DMA((3,)),
        pltpu.SemaphoreType.DMA((1,)),
        pltpu.SemaphoreType.DMA((1,)),
        pltpu.SemaphoreType.DMA((1,)),
        pltpu.SemaphoreType.DMA((1,)),
        pltpu.SemaphoreType.DMA((nr // 2,)),
        pltpu.SemaphoreType.DMA((nr // 2,)),
        pltpu.SemaphoreType.DMA((1,)),
        pltpu.SemaphoreType.DMA((1,)),
    ]
    base, last = pl.pallas_call(
        functools.partial(kernel, nr, nj),
        out_shape=(jax.ShapeDtypeStruct(trial.shape, F32),) * 2,
        in_specs=[pl.BlockSpec(memory_space=pltpu.HBM)] * 6,
        out_specs=(pl.BlockSpec(memory_space=pltpu.HBM), pl.BlockSpec(memory_space=pltpu.VMEM)),
        scratch_shapes=scratch,
        compiler_params=pltpu.CompilerParams(
            collective_id=0, has_side_effects=True, vmem_limit_bytes=64 * 2**20 - 65536),
    )(trial, screened, val_points, cond_points.reshape(nq, nk, cw), eps_val[None], eps_cond[None])
    return base + last


def fits(nr, nj, trial, val_points, cond_points):
    mb, nv = val_points.shape
    nb, cw = cond_points.shape
    if nr % 2 or nj % 2 or (2 * nr) % nj or nb % (2 * nr // nj):
        return False
    nk = nb // (2 * nr // nj)
    return (trial.shape[0] == 1 and cw == LANES and nk % ROWS16 == 0
            and mb % ROWS16 == 0 and mb <= LANES and nv == 2 * LANES)


def general(trial, screened, val_points, cond_points, eps_val, eps_cond):
    cond_full = lax.all_gather(cond_points, "row", axis=1, tiled=True)
    energy_full = eps_cond[None, :] - eps_val[:, None]
    width = trial.shape[2]
    offset = lax.axis_index("row") * width
    x_full = lax.all_gather(trial.astype(BF16), "row", axis=2, tiled=True).astype(trial.dtype)
    xb_full = x_full.astype(BF16)
    x_mine = trial
    for step in range(APPLY):
        pair = jnp.einsum(
            "mv,bvc->bmc", val_points, xb_full, preferred_element_type=F32).astype(BF16)
        inner = jnp.einsum("bmc,nc->bmn", pair, cond_full, preferred_element_type=F32)
        tile = (screened[None] * inner).astype(BF16)
        back = jnp.einsum("bmn,nc->bmc", tile, cond_full, preferred_element_type=F32).astype(BF16)
        part_low = jnp.einsum(
            "mv,bmc->bvc", val_points, back, preferred_element_type=F32).astype(BF16)
        partial_terms = lax.optimization_barrier(part_low).astype(F32)
        kernel_full = lax.psum(partial_terms, ("row", "col"))
        x_full = energy_full[None] * x_full + kernel_full
        xb_full = x_full.astype(BF16)
        x_mine = lax.dynamic_slice_in_dim(x_full, offset, width, 2)
    return x_mine


def solution(mesh):
    nr, nj = mesh.shape["row"], mesh.shape["col"]

    def body(trial, screened, val_points, cond_points, eps_val, eps_cond):
        args = (trial, screened, val_points, cond_points, eps_val, eps_cond)
        if fits(nr, nj, trial, val_points, cond_points):
            return fused(nr, nj, *args)
        return general(*args)

    in_specs = (P(None, None, "row"), P("row", "col"), P("row", None), P("col", "row"), P(), P())
    out_specs = P(None, None, "row")
    return jax.shard_map(body, mesh=mesh, in_specs=in_specs, out_specs=out_specs, check_vma=False)
```

```python
import functools

import jax
import jax.numpy as jnp
from jax import lax
from jax.experimental import pallas as pl
from jax.experimental.pallas import tpu as pltpu
from jax.sharding import PartitionSpec as P

APPLY = 2
LANES = 128
ROWS16 = 16
F32 = jnp.float32
BF16 = jnp.bfloat16
MESH = pl.DeviceIdType.MESH


def dot_nt(a, b):
    return lax.dot_general(a, b, (((1,), (1,)), ((), ())), preferred_element_type=F32)


def kernel(nr, nj, x_hbm, s_hbm, v_hbm, c_hbm, ev_hbm, ec_hbm, out_ref,
           xv, sv, cv, evv, ecv, vall, st, sall, asend, arecv, call, evb,
           ysend0, ysend1, yall0, yall1, esend, erecv, kz0, w0, b1t, condt,
           local_sem, own_send, own_recv, col_send, col_recv, peer_send, peer_recv,
           mate_send, mate_recv, far_send, far_recv,
           val_send, val_recv, pass_send, pass_recv):
    r = lax.axis_index("row")
    j = lax.axis_index("col")
    group, plane = j // 2, lax.rem(j, 2)
    me = r * 2 + plane
    np = nr * 2
    nq = np // nj
    mb, nv = v_hbm.shape
    _, nk, cw = c_hbm.shape
    nb = nq * nk
    vh = nv // 2

    loads = {}

    def load(names):
        for name, src, dst in names:
            loads[name] = pltpu.make_async_copy(src, dst, local_sem.at[len(loads)])
            loads[name].start()

    load([("c", c_hbm, cv), ("x", x_hbm, xv)])
    barrier = pltpu.get_barrier_semaphore()
    steps = sorted(range(1, np), key=lambda k: abs(k - np // 2))
    peers = [lax.rem(me + k, np) for k in steps]
    chips = [lax.rem(r + 2 * k, nr) for k in range(1, nr // 2)]
    mate = r + 1 - 2 * lax.rem(r, 2)
    col_peers = [lax.rem(j + k, nj) for k in range(1, nj)]
    far_groups = [lax.rem(group + k, nj // 2) for k in range(1, nj // 2)]
    for p in peers:
        pl.semaphore_signal(barrier, inc=1, device_id=(p // 2, group * 2 + lax.rem(p, 2)),
                            device_id_type=MESH)
    for g in far_groups:
        for s in range(nr):
            pl.semaphore_signal(barrier, inc=1, device_id=(s, g * 2 + plane),
                                device_id_type=MESH)
        pl.semaphore_signal(barrier, inc=1, device_id=(r, g * 2 + 1 - plane),
                            device_id_type=MESH)
    greeted = np - 1 + (nj // 2 - 1) * (nr + 1)

    load([("v", v_hbm, vall.at[r, pl.ds(0, mb)]), ("s", s_hbm, sv), ("ev", ev_hbm, evv),
          ("ec", ec_hbm, ecv), ("call", c_hbm, call.at[:, j])])

    def remote(src, dst, send_sem, recv_sem, row, col):
        return pltpu.make_async_remote_copy(
            src_ref=src, dst_ref=dst, send_sem=send_sem, recv_sem=recv_sem,
            device_id=(row, col), device_id_type=MESH)

    def arrived(ref, sem):
        remote(ref, ref, col_send.at[0], sem, mate, j).wait_recv()

    def sent(ref, sem):
        remote(ref, ref, sem, col_recv.at[0], mate, j).wait_send()

    def val_block(s):
        return vall.at[s, pl.ds(0, mb)]

    def val_copy(s):
        return remote(v_hbm, val_block(r), val_send.at[s // 2], val_recv.at[r // 2], s, j)

    def pass_copy(s):
        return remote(val_block(s), val_block(s), pass_send.at[0], pass_recv.at[0], mate, j)

    def peer_copy(phase, src, dst, peer):
        return remote(src, dst, peer_send.at[phase], peer_recv.at[phase],
                      peer // 2, group * 2 + lax.rem(peer, 2))

    def owner_copy(phase, src, dst, q, g):
        return remote(src, dst, own_send.at[phase], own_recv.at[phase],
                      q * (nj // 2) + group, g * 2 + plane)

    groups = [lax.rem(group + k, nj // 2) for k in range(nj // 2)]

    def owner_each(q, g, away, here):
        if g is groups[0]:
            itself = q * (nj // 2) + group == r
            pl.when(jnp.logical_not(itself))(away)
            if here is not None:
                pl.when(itself)(here)
        else:
            away()

    def owner_send(phase, buffer, target, chosen):
        for g in chosen:
            for q in range(nq):
                def away():
                    owner_copy(phase, buffer.at[q], target.at[r], q, g).start()

                def here():
                    target[r] = buffer[q]

                owner_each(q, g, away, here)

    holder = lax.rem(r, nj // 2) * 2 + plane
    holds = holder == j

    def far_copy(g):
        return remote(w0, w0, far_send.at[0], far_recv.at[0], r, g * 2 + plane)

    def all_send(phase, src_of, dst):
        for p in peers:
            peer_copy(phase, src_of(p), dst, p).start()

    loads["c"].wait()
    loads["x"].wait()
    first = dot_nt(cv[...].reshape(nb, cw), xv[0].astype(BF16))
    asend[...] = first.astype(BF16).reshape(asend.shape)

    pl.semaphore_wait(barrier, greeted)
    owner_send(0, asend, arecv, groups[:1])
    for s in chips:
        val_copy(s).start()
    loads["v"].wait()
    pass_copy(r).start()

    loads["s"].wait()
    scr = sv[...].astype(F32)
    scr = jnp.concatenate([scr, jnp.zeros((LANES - mb, nb), F32)], axis=0)
    wide = -(-nb // LANES) * LANES
    if wide > nb:
        scr = jnp.concatenate([scr, jnp.zeros((LANES, wide - nb), F32)], axis=1)
    scr = scr.T
    st[...] = scr[:nb].astype(BF16).reshape(st.shape)
    owner_send(1, st, sall, groups[1:] + groups[:1])
    for s in col_peers:
        remote(c_hbm, call.at[:, j], col_send.at[0], col_recv.at[0], r, s).start()

    if mb < LANES:
        for i in range(nr):
            vall[i, pl.ds(mb, LANES - mb)] = jnp.zeros((LANES - mb, nv), BF16)
    for name in ("ev", "ec", "call"):
        loads[name].wait()
    evb[...] = jnp.broadcast_to(evv[...], (LANES, nv)).T
    ec = ecv[:, pl.ds(pl.multiple_of(r * cw, cw), cw)]

    def screen(w):
        allv = vall[...].reshape(nr * LANES, nv)
        inner = dot_nt(w, allv)
        tile = jnp.concatenate(
            [(sall[i].astype(F32) * inner[:, i * LANES:(i + 1) * LANES]).astype(BF16)
             for i in range(nr)], axis=1)
        return jnp.dot(tile, allv, preferred_element_type=F32).astype(BF16)

    mine = pl.ds(pl.multiple_of(plane * vh, vh), vh)
    b1t[...] = ((ec - evb[mine, :]) * xv[0, mine, :]).T

    @pl.when(holds)
    def _():
        arrived(arecv.at[pl.ds(0, nr - 1)], own_recv.at[0])
        total = arecv[0].astype(F32)
        for i in range(1, nr):
            total = total + arecv[i].astype(F32)
        w0[...] = total.astype(BF16)
        for g in groups[1:]:
            far_copy(g).start()

    for s in reversed(chips):
        arrived(val_block(s), val_recv.at[s // 2])
        pass_copy(s).start()

    @pl.when(holds)
    def _():
        arrived(sall.at[pl.ds(0, nr - 1)], own_recv.at[1])

    @pl.when(jnp.logical_not(holds))
    def _():
        arrived(sall, own_recv.at[1])
        arrived(w0, far_recv.at[0])

    arrived(vall.at[pl.ds(0, nr // 2), pl.ds(0, mb)], pass_recv.at[0])
    y0 = screen(w0[...])
    ysend0[0] = y0[:, :vh]
    ysend0[1] = y0[:, vh:]
    all_send(0, lambda p: ysend0.at[lax.rem(p, 2)], yall0.at[me])
    yall0[me] = ysend0[plane]
    arrived(call.at[:, pl.ds(0, nj - 1)], col_recv.at[0])
    condt[...] = call[...].reshape(np * nk, cw).T
    for s in chips:
        val_copy(s).wait_send()
    sent(vall.at[pl.ds(0, nr // 2), pl.ds(0, mb)], pass_send.at[0])
    sent(call.at[:, pl.ds(0, nj - 1)], col_send.at[0])

    @pl.when(holds)
    def _():
        sent(asend.at[pl.ds(0, nq - 1)], own_send.at[0])
        sent(sall.at[pl.ds(0, nr - 1)], own_send.at[1])
        sent(arecv.at[pl.ds(0, nj // 2 - 1)], far_send.at[0])

    @pl.when(jnp.logical_not(holds))
    def _():
        sent(asend, own_send.at[0])
        sent(sall, own_send.at[1])

    arrived(yall0.at[pl.ds(0, np - 1)], peer_recv.at[0])
    k0t = jnp.dot(condt[...], yall0[...].reshape(np * nk, vh), preferred_element_type=F32)
    x1t = (b1t[...] + k0t).astype(BF16)

    def kernel_block(p):
        cond = call[p // nj, lax.rem(p, nj)]
        esend[p] = jnp.dot(cond, x1t, preferred_element_type=F32).astype(BF16)

    for p in peers:
        kernel_block(p)
        peer_copy(1, esend.at[p], erecv.at[plane * nr + r], p).start()
    kernel_block(me)
    erecv[plane * nr + r] = esend[me]
    kz0[plane] = k0t.astype(BF16)

    other = group * 2 + 1 - plane
    swap = remote(kz0.at[plane], kz0.at[plane], mate_send.at[0], mate_recv.at[0], r, other)
    swap.start()
    sent(yall0.at[pl.ds(0, np - 1)], peer_send.at[0])
    arrived(erecv.at[pl.ds(0, np - 1)], peer_recv.at[1])

    halves = []
    for h in range(2):
        total = erecv[h * nr].astype(F32)
        for i in range(1, nr):
            total = total + erecv[h * nr + i].astype(F32)
        halves.append(total)
    ysend1[...] = screen(jnp.concatenate(halves, axis=1).astype(BF16))
    all_send(2, lambda p: ysend1, yall1.at[me])
    yall1[me] = ysend1[...]
    arrived(kz0.at[1 - plane], mate_recv.at[0])
    energy = ec - evb[...]
    k0 = jnp.concatenate([kz0[h].astype(F32).T for h in range(2)], axis=0)
    out_ref[0] = energy * (energy * xv[0] + k0)
    swap.wait_send()
    sent(erecv.at[pl.ds(0, np - 1)], peer_send.at[1])
    arrived(yall1.at[pl.ds(0, np - 1)], peer_recv.at[2])
    k1t = jnp.dot(condt[...], yall1[...].reshape(np * nk, nv), preferred_element_type=F32)
    out_ref[0] += k1t.T
    sent(yall1.at[pl.ds(0, np - 1)], peer_send.at[2])


def fused(nr, nj, trial, screened, val_points, cond_points, eps_val, eps_cond):
    mb, nv = val_points.shape
    nb, cw = cond_points.shape
    np = 2 * nr
    nq = np // nj
    nk = nb // nq
    vh = nv // 2
    ng = nj // 2
    scratch = [
        pltpu.VMEM(trial.shape, F32),
        pltpu.VMEM(screened.shape, BF16),
        pltpu.VMEM((nq, nk, cw), BF16),
        pltpu.VMEM((1, nv), F32),
        pltpu.VMEM((1, eps_cond.shape[0]), F32),
        pltpu.VMEM((nr, LANES, nv), BF16),
        pltpu.VMEM((nq, nk, LANES), BF16),
        pltpu.VMEM((nr, nk, LANES), BF16),
        pltpu.VMEM((nq, nk, nv), BF16),
        pltpu.VMEM((nr, nk, nv), BF16),
        pltpu.VMEM((nq, nj, nk, cw), BF16),
        pltpu.VMEM((nv, LANES), F32),
        pltpu.VMEM((2, nk, vh), BF16),
        pltpu.VMEM((nk, nv), BF16),
        pltpu.VMEM((np, nk, vh), BF16),
        pltpu.VMEM((np, nk, nv), BF16),
        pltpu.VMEM((np, nk, vh), BF16),
        pltpu.VMEM((np, nk, vh), BF16),
        pltpu.VMEM((2, cw, vh), BF16),
        pltpu.VMEM((nk, nv), BF16),
        pltpu.VMEM((cw, vh), F32),
        pltpu.VMEM((cw, np * nk), BF16),
        pltpu.SemaphoreType.DMA((7,)),
        pltpu.SemaphoreType.DMA((2,)),
        pltpu.SemaphoreType.DMA((2,)),
        pltpu.SemaphoreType.DMA((1,)),
        pltpu.SemaphoreType.DMA((1,)),
        pltpu.SemaphoreType.DMA((3,)),
        pltpu.SemaphoreType.DMA((3,)),
        pltpu.SemaphoreType.DMA((1,)),
        pltpu.SemaphoreType.DMA((1,)),
        pltpu.SemaphoreType.DMA((1,)),
        pltpu.SemaphoreType.DMA((1,)),
        pltpu.SemaphoreType.DMA((nr // 2,)),
        pltpu.SemaphoreType.DMA((nr // 2,)),
        pltpu.SemaphoreType.DMA((1,)),
        pltpu.SemaphoreType.DMA((1,)),
    ]
    return pl.pallas_call(
        functools.partial(kernel, nr, nj),
        out_shape=pltpu.VMEM(trial.shape, F32),
        in_specs=[pl.BlockSpec(memory_space=pltpu.HBM)] * 6,
        out_specs=pl.BlockSpec(memory_space=pltpu.VMEM),
        scratch_shapes=scratch,
        compiler_params=pltpu.CompilerParams(
            collective_id=0, has_side_effects=True, vmem_limit_bytes=64 * 2**20 - 2**18),
    )(trial, screened, val_points, cond_points.reshape(nq, nk, cw), eps_val[None], eps_cond[None])


def fits(nr, nj, trial, val_points, cond_points):
    mb, nv = val_points.shape
    nb, cw = cond_points.shape
    if nr % 2 or nj % 2 or (2 * nr) % nj or nb % (2 * nr // nj):
        return False
    nk = nb // (2 * nr // nj)
    return (trial.shape[0] == 1 and cw == LANES and nk % ROWS16 == 0
            and mb % ROWS16 == 0 and mb <= LANES and nv == 2 * LANES)


def general(trial, screened, val_points, cond_points, eps_val, eps_cond):
    cond_full = lax.all_gather(cond_points, "row", axis=1, tiled=True)
    energy_full = eps_cond[None, :] - eps_val[:, None]
    width = trial.shape[2]
    offset = lax.axis_index("row") * width
    x_full = lax.all_gather(trial.astype(BF16), "row", axis=2, tiled=True).astype(trial.dtype)
    xb_full = x_full.astype(BF16)
    x_mine = trial
    for step in range(APPLY):
        pair = jnp.einsum(
            "mv,bvc->bmc", val_points, xb_full, preferred_element_type=F32).astype(BF16)
        inner = jnp.einsum("bmc,nc->bmn", pair, cond_full, preferred_element_type=F32)
        tile = (screened[None] * inner).astype(BF16)
        back = jnp.einsum("bmn,nc->bmc", tile, cond_full, preferred_element_type=F32).astype(BF16)
        part_low = jnp.einsum(
            "mv,bmc->bvc", val_points, back, preferred_element_type=F32).astype(BF16)
        partial_terms = lax.optimization_barrier(part_low).astype(F32)
        kernel_full = lax.psum(partial_terms, ("row", "col"))
        x_full = energy_full[None] * x_full + kernel_full
        xb_full = x_full.astype(BF16)
        x_mine = lax.dynamic_slice_in_dim(x_full, offset, width, 2)
    return x_mine


def solution(mesh):
    nr, nj = mesh.shape["row"], mesh.shape["col"]

    def body(trial, screened, val_points, cond_points, eps_val, eps_cond):
        args = (trial, screened, val_points, cond_points, eps_val, eps_cond)
        if fits(nr, nj, trial, val_points, cond_points):
            return fused(nr, nj, *args)
        return general(*args)

    in_specs = (P(None, None, "row"), P("row", "col"), P("row", None), P("col", "row"), P(), P())
    out_specs = P(None, None, "row")
    return jax.shard_map(body, mesh=mesh, in_specs=in_specs, out_specs=out_specs, check_vma=False)
```

```python
import functools

import jax
import jax.numpy as jnp
from jax import lax
from jax.experimental import pallas as pl
from jax.experimental.pallas import tpu as pltpu
from jax.sharding import PartitionSpec as P

APPLY = 2
LANES = 128
ROWS16 = 16
F32 = jnp.float32
BF16 = jnp.bfloat16
MESH = pl.DeviceIdType.MESH


def dot_nt(a, b):
    return lax.dot_general(a, b, (((1,), (1,)), ((), ())), preferred_element_type=F32)


def kernel(nr, nj, x_hbm, s_hbm, v_hbm, c_hbm, ev_hbm, ec_hbm, out_ref,
           xv, sv, cv, evv, ecv, vall, st, sall, asend, arecv, call, evb,
           ysend0, ysend1, yall0, yall1, esend, erecv, kz0, w0, b1t, condt,
           local_sem, own_send, own_recv, col_send, col_recv, peer_send, peer_recv,
           mate_send, mate_recv, far_send, far_recv,
           val_send, val_recv, pass_send, pass_recv):
    r = lax.axis_index("row")
    j = lax.axis_index("col")
    group, plane = j // 2, lax.rem(j, 2)
    me = r * 2 + plane
    np = nr * 2
    nq = np // nj
    mb, nv = v_hbm.shape
    _, nk, cw = c_hbm.shape
    nb = nq * nk
    vh = nv // 2

    loads = {}

    def load(names):
        for name, src, dst in names:
            loads[name] = pltpu.make_async_copy(src, dst, local_sem.at[len(loads)])
            loads[name].start()

    load([("c", c_hbm, cv), ("x", x_hbm, xv)])
    barrier = pltpu.get_barrier_semaphore()
    steps = sorted(range(1, np), key=lambda k: abs(k - np // 2))
    peers = [lax.rem(me + k, np) for k in steps]
    chips = [lax.rem(r + 2 * k, nr) for k in range(1, nr // 2)]
    mate = r + 1 - 2 * lax.rem(r, 2)
    col_peers = [lax.rem(j + k, nj) for k in range(1, nj)]
    far_groups = [lax.rem(group + k, nj // 2) for k in range(1, nj // 2)]
    for p in peers:
        pl.semaphore_signal(barrier, inc=1, device_id=(p // 2, group * 2 + lax.rem(p, 2)),
                            device_id_type=MESH)
    for g in far_groups:
        for s in range(nr):
            pl.semaphore_signal(barrier, inc=1, device_id=(s, g * 2 + plane),
                                device_id_type=MESH)
        pl.semaphore_signal(barrier, inc=1, device_id=(r, g * 2 + 1 - plane),
                            device_id_type=MESH)
    greeted = np - 1 + (nj // 2 - 1) * (nr + 1)

    load([("v", v_hbm, vall.at[r, pl.ds(0, mb)]), ("s", s_hbm, sv), ("ev", ev_hbm, evv),
          ("ec", ec_hbm, ecv), ("call", c_hbm, call.at[:, j])])

    def remote(src, dst, send_sem, recv_sem, row, col):
        return pltpu.make_async_remote_copy(
            src_ref=src, dst_ref=dst, send_sem=send_sem, recv_sem=recv_sem,
            device_id=(row, col), device_id_type=MESH)

    def arrived(ref, sem):
        remote(ref, ref, col_send.at[0], sem, mate, j).wait_recv()

    def sent(ref, sem):
        remote(ref, ref, sem, col_recv.at[0], mate, j).wait_send()

    def val_block(s):
        return vall.at[s, pl.ds(0, mb)]

    def val_copy(s):
        return remote(v_hbm, val_block(r), val_send.at[s // 2], val_recv.at[r // 2], s, j)

    def pass_copy(s):
        return remote(val_block(s), val_block(s), pass_send.at[0], pass_recv.at[0], mate, j)

    def peer_copy(phase, src, dst, peer):
        return remote(src, dst, peer_send.at[phase], peer_recv.at[phase],
                      peer // 2, group * 2 + lax.rem(peer, 2))

    def owner_copy(phase, src, dst, q, g):
        return remote(src, dst, own_send.at[phase], own_recv.at[phase],
                      q * (nj // 2) + group, g * 2 + plane)

    groups = [lax.rem(group + k, nj // 2) for k in range(nj // 2)]

    def owner_each(q, g, away, here):
        if g is groups[0]:
            itself = q * (nj // 2) + group == r
            pl.when(jnp.logical_not(itself))(away)
            if here is not None:
                pl.when(itself)(here)
        else:
            away()

    def owner_send(phase, buffer, target, chosen):
        for g in chosen:
            for q in range(nq):
                def away():
                    owner_copy(phase, buffer.at[q], target.at[r], q, g).start()

                def here():
                    target[r] = buffer[q]

                owner_each(q, g, away, here)

    holder = lax.rem(r, nj // 2) * 2 + plane
    holds = holder == j

    def far_copy(g):
        return remote(w0, w0, far_send.at[0], far_recv.at[0], r, g * 2 + plane)

    def all_send(phase, src_of, dst):
        for p in peers:
            peer_copy(phase, src_of(p), dst, p).start()

    loads["c"].wait()
    loads["x"].wait()
    first = dot_nt(cv[...].reshape(nb, cw), xv[0].astype(BF16))
    asend[...] = first.astype(BF16).reshape(asend.shape)

    pl.semaphore_wait(barrier, greeted)
    owner_send(0, asend, arecv, groups[:1])
    for s in chips:
        val_copy(s).start()
    loads["v"].wait()
    pass_copy(r).start()

    loads["s"].wait()
    scr = sv[...].astype(F32)
    scr = jnp.concatenate([scr, jnp.zeros((LANES - mb, nb), F32)], axis=0)
    wide = -(-nb // LANES) * LANES
    if wide > nb:
        scr = jnp.concatenate([scr, jnp.zeros((LANES, wide - nb), F32)], axis=1)
    scr = scr.T
    st[...] = scr[:nb].astype(BF16).reshape(st.shape)
    owner_send(1, st, sall, groups[1:] + groups[:1])
    for s in col_peers:
        remote(c_hbm, call.at[:, j], col_send.at[0], col_recv.at[0], r, s).start()

    if mb < LANES:
        for i in range(nr):
            vall[i, pl.ds(mb, LANES - mb)] = jnp.zeros((LANES - mb, nv), BF16)
    for name in ("ev", "ec", "call"):
        loads[name].wait()
    evb[...] = jnp.broadcast_to(evv[...], (LANES, nv)).T
    ec = ecv[:, pl.ds(pl.multiple_of(r * cw, cw), cw)]

    def screen(w):
        allv = vall[...].reshape(nr * LANES, nv)
        inner = dot_nt(w, allv)
        tile = jnp.concatenate(
            [(sall[i].astype(F32) * inner[:, i * LANES:(i + 1) * LANES]).astype(BF16)
             for i in range(nr)], axis=1)
        return jnp.dot(tile, allv, preferred_element_type=F32).astype(BF16)

    mine = pl.ds(pl.multiple_of(plane * vh, vh), vh)
    b1t[...] = ((ec - evb[mine, :]) * xv[0, mine, :]).T

    @pl.when(holds)
    def _():
        arrived(arecv.at[pl.ds(0, nr - 1)], own_recv.at[0])
        total = arecv[0].astype(F32)
        for i in range(1, nr):
            total = total + arecv[i].astype(F32)
        w0[...] = total.astype(BF16)
        for g in groups[1:]:
            far_copy(g).start()

    for s in reversed(chips):
        arrived(val_block(s), val_recv.at[s // 2])
        pass_copy(s).start()

    @pl.when(holds)
    def _():
        arrived(sall.at[pl.ds(0, nr - 1)], own_recv.at[1])

    @pl.when(jnp.logical_not(holds))
    def _():
        arrived(sall, own_recv.at[1])
        arrived(w0, far_recv.at[0])

    arrived(vall.at[pl.ds(0, nr // 2), pl.ds(0, mb)], pass_recv.at[0])
    y0 = screen(w0[...])
    ysend0[0] = y0[:, :vh]
    ysend0[1] = y0[:, vh:]
    all_send(0, lambda p: ysend0.at[lax.rem(p, 2)], yall0.at[me])
    yall0[me] = ysend0[plane]
    arrived(call.at[:, pl.ds(0, nj - 1)], col_recv.at[0])
    condt[...] = call[...].reshape(np * nk, cw).T
    for s in chips:
        val_copy(s).wait_send()
    sent(vall.at[pl.ds(0, nr // 2), pl.ds(0, mb)], pass_send.at[0])
    sent(call.at[:, pl.ds(0, nj - 1)], col_send.at[0])

    @pl.when(holds)
    def _():
        sent(asend.at[pl.ds(0, nq - 1)], own_send.at[0])
        sent(sall.at[pl.ds(0, nr - 1)], own_send.at[1])
        sent(arecv.at[pl.ds(0, nj // 2 - 1)], far_send.at[0])

    @pl.when(jnp.logical_not(holds))
    def _():
        sent(asend, own_send.at[0])
        sent(sall, own_send.at[1])

    arrived(yall0.at[pl.ds(0, np - 1)], peer_recv.at[0])
    k0t = jnp.dot(condt[...], yall0[...].reshape(np * nk, vh), preferred_element_type=F32)
    x1t = (b1t[...] + k0t).astype(BF16)

    cond = call[...].reshape(np * nk, cw)
    esend[...] = jnp.dot(cond, x1t, preferred_element_type=F32).astype(BF16).reshape(esend.shape)
    all_send(1, lambda p: esend.at[p], erecv.at[plane * nr + r])
    erecv[plane * nr + r] = esend[me]
    kz0[plane] = k0t.astype(BF16)

    other = group * 2 + 1 - plane
    swap = remote(kz0.at[plane], kz0.at[plane], mate_send.at[0], mate_recv.at[0], r, other)
    swap.start()
    sent(yall0.at[pl.ds(0, np - 1)], peer_send.at[0])
    arrived(erecv.at[pl.ds(0, np - 1)], peer_recv.at[1])

    halves = []
    for h in range(2):
        total = erecv[h * nr].astype(F32)
        for i in range(1, nr):
            total = total + erecv[h * nr + i].astype(F32)
        halves.append(total)
    ysend1[...] = screen(jnp.concatenate(halves, axis=1).astype(BF16))
    all_send(2, lambda p: ysend1, yall1.at[me])
    yall1[me] = ysend1[...]
    arrived(kz0.at[1 - plane], mate_recv.at[0])
    energy = ec - evb[...]
    k0 = jnp.concatenate([kz0[h].astype(F32).T for h in range(2)], axis=0)
    out_ref[0] = energy * (energy * xv[0] + k0)
    swap.wait_send()
    sent(erecv.at[pl.ds(0, np - 1)], peer_send.at[1])
    arrived(yall1.at[pl.ds(0, np - 1)], peer_recv.at[2])
    k1t = jnp.dot(condt[...], yall1[...].reshape(np * nk, nv), preferred_element_type=F32)
    out_ref[0] += k1t.T
    sent(yall1.at[pl.ds(0, np - 1)], peer_send.at[2])


def fused(nr, nj, trial, screened, val_points, cond_points, eps_val, eps_cond):
    mb, nv = val_points.shape
    nb, cw = cond_points.shape
    np = 2 * nr
    nq = np // nj
    nk = nb // nq
    vh = nv // 2
    ng = nj // 2
    scratch = [
        pltpu.VMEM(trial.shape, F32),
        pltpu.VMEM(screened.shape, BF16),
        pltpu.VMEM((nq, nk, cw), BF16),
        pltpu.VMEM((1, nv), F32),
        pltpu.VMEM((1, eps_cond.shape[0]), F32),
        pltpu.VMEM((nr, LANES, nv), BF16),
        pltpu.VMEM((nq, nk, LANES), BF16),
        pltpu.VMEM((nr, nk, LANES), BF16),
        pltpu.VMEM((nq, nk, nv), BF16),
        pltpu.VMEM((nr, nk, nv), BF16),
        pltpu.VMEM((nq, nj, nk, cw), BF16),
        pltpu.VMEM((nv, LANES), F32),
        pltpu.VMEM((2, nk, vh), BF16),
        pltpu.VMEM((nk, nv), BF16),
        pltpu.VMEM((np, nk, vh), BF16),
        pltpu.VMEM((np, nk, nv), BF16),
        pltpu.VMEM((np, nk, vh), BF16),
        pltpu.VMEM((np, nk, vh), BF16),
        pltpu.VMEM((2, cw, vh), BF16),
        pltpu.VMEM((nk, nv), BF16),
        pltpu.VMEM((cw, vh), F32),
        pltpu.VMEM((cw, np * nk), BF16),
        pltpu.SemaphoreType.DMA((7,)),
        pltpu.SemaphoreType.DMA((2,)),
        pltpu.SemaphoreType.DMA((2,)),
        pltpu.SemaphoreType.DMA((1,)),
        pltpu.SemaphoreType.DMA((1,)),
        pltpu.SemaphoreType.DMA((3,)),
        pltpu.SemaphoreType.DMA((3,)),
        pltpu.SemaphoreType.DMA((1,)),
        pltpu.SemaphoreType.DMA((1,)),
        pltpu.SemaphoreType.DMA((1,)),
        pltpu.SemaphoreType.DMA((1,)),
        pltpu.SemaphoreType.DMA((nr // 2,)),
        pltpu.SemaphoreType.DMA((nr // 2,)),
        pltpu.SemaphoreType.DMA((1,)),
        pltpu.SemaphoreType.DMA((1,)),
    ]
    return pl.pallas_call(
        functools.partial(kernel, nr, nj),
        out_shape=pltpu.VMEM(trial.shape, F32),
        in_specs=[pl.BlockSpec(memory_space=pltpu.HBM)] * 6,
        out_specs=pl.BlockSpec(memory_space=pltpu.VMEM),
        scratch_shapes=scratch,
        compiler_params=pltpu.CompilerParams(
            collective_id=0, has_side_effects=True, vmem_limit_bytes=64 * 2**20 - 2**18),
    )(trial, screened, val_points, cond_points.reshape(nq, nk, cw), eps_val[None], eps_cond[None])


def fits(nr, nj, trial, val_points, cond_points):
    mb, nv = val_points.shape
    nb, cw = cond_points.shape
    if nr % 2 or nj % 2 or (2 * nr) % nj or nb % (2 * nr // nj):
        return False
    nk = nb // (2 * nr // nj)
    return (trial.shape[0] == 1 and cw == LANES and nk % ROWS16 == 0
            and mb % ROWS16 == 0 and mb <= LANES and nv == 2 * LANES)


def general(trial, screened, val_points, cond_points, eps_val, eps_cond):
    cond_full = lax.all_gather(cond_points, "row", axis=1, tiled=True)
    energy_full = eps_cond[None, :] - eps_val[:, None]
    width = trial.shape[2]
    offset = lax.axis_index("row") * width
    x_full = lax.all_gather(trial.astype(BF16), "row", axis=2, tiled=True).astype(trial.dtype)
    xb_full = x_full.astype(BF16)
    x_mine = trial
    for step in range(APPLY):
        pair = jnp.einsum(
            "mv,bvc->bmc", val_points, xb_full, preferred_element_type=F32).astype(BF16)
        inner = jnp.einsum("bmc,nc->bmn", pair, cond_full, preferred_element_type=F32)
        tile = (screened[None] * inner).astype(BF16)
        back = jnp.einsum("bmn,nc->bmc", tile, cond_full, preferred_element_type=F32).astype(BF16)
        part_low = jnp.einsum(
            "mv,bmc->bvc", val_points, back, preferred_element_type=F32).astype(BF16)
        partial_terms = lax.optimization_barrier(part_low).astype(F32)
        kernel_full = lax.psum(partial_terms, ("row", "col"))
        x_full = energy_full[None] * x_full + kernel_full
        xb_full = x_full.astype(BF16)
        x_mine = lax.dynamic_slice_in_dim(x_full, offset, width, 2)
    return x_mine


def solution(mesh):
    nr, nj = mesh.shape["row"], mesh.shape["col"]

    def body(trial, screened, val_points, cond_points, eps_val, eps_cond):
        args = (trial, screened, val_points, cond_points, eps_val, eps_cond)
        if fits(nr, nj, trial, val_points, cond_points):
            return fused(nr, nj, *args)
        return general(*args)

    in_specs = (P(None, None, "row"), P("row", "col"), P("row", None), P("col", "row"), P(), P())
    out_specs = P(None, None, "row")
    return jax.shard_map(body, mesh=mesh, in_specs=in_specs, out_specs=out_specs, check_vma=False)
```

```python
import functools

import jax
import jax.numpy as jnp
from jax import lax
from jax.experimental import pallas as pl
from jax.experimental.pallas import tpu as pltpu
from jax.sharding import PartitionSpec as P

APPLY = 2
LANES = 128
ROWS16 = 16
F32 = jnp.float32
BF16 = jnp.bfloat16
MESH = pl.DeviceIdType.MESH


def dot_nt(a, b):
    return lax.dot_general(a, b, (((1,), (1,)), ((), ())), preferred_element_type=F32)


def kernel(nr, nj, x_hbm, s_hbm, v_hbm, c_hbm, ev_hbm, ec_hbm, out_ref,
           xv, sv, cv, evv, ecv, vall, st, sall, asend, arecv, call, evb,
           ysend0, ysend1, yall0, yall1, esend, erecv, kz0, w0, b1t, condt,
           local_sem, own_send, own_recv, col_send, col_recv, peer_send, peer_recv,
           mate_send, mate_recv, far_send, far_recv,
           val_send, val_recv, pass_send, pass_recv,
           last_send, last_recv, hand_send, hand_recv):
    r = lax.axis_index("row")
    j = lax.axis_index("col")
    group, plane = j // 2, lax.rem(j, 2)
    me = r * 2 + plane
    np = nr * 2
    nq = np // nj
    mb, nv = v_hbm.shape
    _, nk, cw = c_hbm.shape
    nb = nq * nk
    vh = nv // 2

    loads = {}

    def load(names):
        for name, src, dst in names:
            loads[name] = pltpu.make_async_copy(src, dst, local_sem.at[len(loads)])
            loads[name].start()

    load([("c", c_hbm, cv), ("x", x_hbm, xv)])
    barrier = pltpu.get_barrier_semaphore()
    steps = sorted(range(1, np), key=lambda k: abs(k - np // 2))
    peers = [lax.rem(me + k, np) for k in steps]
    chips = [lax.rem(r + 2 * k, nr) for k in range(1, nr // 2)]
    mate = r + 1 - 2 * lax.rem(r, 2)
    col_peers = [lax.rem(j + k, nj) for k in range(1, nj)]
    far_groups = [lax.rem(group + k, nj // 2) for k in range(1, nj // 2)]
    for p in peers:
        pl.semaphore_signal(barrier, inc=1, device_id=(p // 2, group * 2 + lax.rem(p, 2)),
                            device_id_type=MESH)
    for g in far_groups:
        for s in range(nr):
            pl.semaphore_signal(barrier, inc=1, device_id=(s, g * 2 + plane),
                                device_id_type=MESH)
        pl.semaphore_signal(barrier, inc=1, device_id=(r, g * 2 + 1 - plane),
                            device_id_type=MESH)
    greeted = np - 1 + (nj // 2 - 1) * (nr + 1)

    load([("v", v_hbm, vall.at[r, pl.ds(0, mb)]), ("s", s_hbm, sv), ("ev", ev_hbm, evv),
          ("ec", ec_hbm, ecv), ("call", c_hbm, call.at[:, j])])

    def remote(src, dst, send_sem, recv_sem, row, col):
        return pltpu.make_async_remote_copy(
            src_ref=src, dst_ref=dst, send_sem=send_sem, recv_sem=recv_sem,
            device_id=(row, col), device_id_type=MESH)

    def arrived(ref, sem):
        remote(ref, ref, col_send.at[0], sem, mate, j).wait_recv()

    def sent(ref, sem):
        remote(ref, ref, sem, col_recv.at[0], mate, j).wait_send()

    def val_block(s):
        return vall.at[s, pl.ds(0, mb)]

    def val_copy(s):
        return remote(v_hbm, val_block(r), val_send.at[s // 2], val_recv.at[r // 2], s, j)

    def pass_copy(s):
        return remote(val_block(s), val_block(s), pass_send.at[0], pass_recv.at[0], mate, j)

    def peer_copy(phase, src, dst, peer):
        return remote(src, dst, peer_send.at[phase], peer_recv.at[phase],
                      peer // 2, group * 2 + lax.rem(peer, 2))

    def owner_copy(phase, src, dst, q, g):
        return remote(src, dst, own_send.at[phase], own_recv.at[phase],
                      q * (nj // 2) + group, g * 2 + plane)

    groups = [lax.rem(group + k, nj // 2) for k in range(nj // 2)]

    def owner_each(q, g, away, here):
        if g is groups[0]:
            itself = q * (nj // 2) + group == r
            pl.when(jnp.logical_not(itself))(away)
            if here is not None:
                pl.when(itself)(here)
        else:
            away()

    def owner_send(phase, buffer, target, chosen):
        for g in chosen:
            for q in range(nq):
                def away():
                    owner_copy(phase, buffer.at[q], target.at[r], q, g).start()

                def here():
                    target[r] = buffer[q]

                owner_each(q, g, away, here)

    holder = lax.rem(r, nj // 2) * 2 + plane
    holds = holder == j

    def far_copy(g):
        return remote(w0, w0, far_send.at[0], far_recv.at[0], r, g * 2 + plane)

    def all_send(phase, src_of, dst):
        for p in peers:
            peer_copy(phase, src_of(p), dst, p).start()

    loads["c"].wait()
    loads["x"].wait()
    first = dot_nt(cv[...].reshape(nb, cw), xv[0].astype(BF16))
    asend[...] = first.astype(BF16).reshape(asend.shape)

    pl.semaphore_wait(barrier, greeted)
    owner_send(0, asend, arecv, groups[:1])
    for s in chips:
        val_copy(s).start()
    loads["v"].wait()
    pass_copy(r).start()

    loads["s"].wait()
    scr = sv[...].astype(F32)
    scr = jnp.concatenate([scr, jnp.zeros((LANES - mb, nb), F32)], axis=0)
    wide = -(-nb // LANES) * LANES
    if wide > nb:
        scr = jnp.concatenate([scr, jnp.zeros((LANES, wide - nb), F32)], axis=1)
    scr = scr.T
    st[...] = scr[:nb].astype(BF16).reshape(st.shape)
    owner_send(1, st, sall, groups[1:] + groups[:1])
    for s in col_peers:
        remote(c_hbm, call.at[:, j], col_send.at[0], col_recv.at[0], r, s).start()

    if mb < LANES:
        for i in range(nr):
            vall[i, pl.ds(mb, LANES - mb)] = jnp.zeros((LANES - mb, nv), BF16)
    for name in ("ev", "ec", "call"):
        loads[name].wait()
    evb[...] = jnp.broadcast_to(evv[...], (LANES, nv)).T
    ec = ecv[:, pl.ds(pl.multiple_of(r * cw, cw), cw)]

    def screen(w):
        allv = vall[...].reshape(nr * LANES, nv)
        inner = dot_nt(w, allv)
        tile = jnp.concatenate(
            [(sall[i].astype(F32) * inner[:, i * LANES:(i + 1) * LANES]).astype(BF16)
             for i in range(nr)], axis=1)
        return jnp.dot(tile, allv, preferred_element_type=F32).astype(BF16)

    mine = pl.ds(pl.multiple_of(plane * vh, vh), vh)
    b1t[...] = ((ec - evb[mine, :]) * xv[0, mine, :]).T

    @pl.when(holds)
    def _():
        arrived(arecv.at[pl.ds(0, nr - 1)], own_recv.at[0])
        total = arecv[0].astype(F32)
        for i in range(1, nr):
            total = total + arecv[i].astype(F32)
        w0[...] = total.astype(BF16)
        for g in groups[1:]:
            far_copy(g).start()

    for s in reversed(chips):
        arrived(val_block(s), val_recv.at[s // 2])
        pass_copy(s).start()

    @pl.when(holds)
    def _():
        arrived(sall.at[pl.ds(0, nr - 1)], own_recv.at[1])

    @pl.when(jnp.logical_not(holds))
    def _():
        arrived(sall, own_recv.at[1])
        arrived(w0, far_recv.at[0])

    arrived(vall.at[pl.ds(0, nr // 2), pl.ds(0, mb)], pass_recv.at[0])
    y0 = screen(w0[...])
    ysend0[0] = y0[:, :vh]
    ysend0[1] = y0[:, vh:]
    all_send(0, lambda p: ysend0.at[lax.rem(p, 2)], yall0.at[me])
    yall0[me] = ysend0[plane]
    arrived(call.at[:, pl.ds(0, nj - 1)], col_recv.at[0])
    condt[...] = call[...].reshape(np * nk, cw).T
    for s in chips:
        val_copy(s).wait_send()
    sent(vall.at[pl.ds(0, nr // 2), pl.ds(0, mb)], pass_send.at[0])
    sent(call.at[:, pl.ds(0, nj - 1)], col_send.at[0])

    @pl.when(holds)
    def _():
        sent(asend.at[pl.ds(0, nq - 1)], own_send.at[0])
        sent(sall.at[pl.ds(0, nr - 1)], own_send.at[1])
        sent(arecv.at[pl.ds(0, nj // 2 - 1)], far_send.at[0])

    @pl.when(jnp.logical_not(holds))
    def _():
        sent(asend, own_send.at[0])
        sent(sall, own_send.at[1])

    arrived(yall0.at[pl.ds(0, np - 1)], peer_recv.at[0])
    k0t = jnp.dot(condt[...], yall0[...].reshape(np * nk, vh), preferred_element_type=F32)
    x1t = (b1t[...] + k0t).astype(BF16)

    cond = call[...].reshape(np * nk, cw)
    esend[...] = jnp.dot(cond, x1t, preferred_element_type=F32).astype(BF16).reshape(esend.shape)
    all_send(1, lambda p: esend.at[p], erecv.at[plane * nr + r])
    erecv[plane * nr + r] = esend[me]
    kz0[plane] = k0t.astype(BF16)

    other = group * 2 + 1 - plane
    swap = remote(kz0.at[plane], kz0.at[plane], mate_send.at[0], mate_recv.at[0], r, other)
    swap.start()
    sent(yall0.at[pl.ds(0, np - 1)], peer_send.at[0])
    arrived(erecv.at[pl.ds(0, np - 1)], peer_recv.at[1])

    halves = []
    for h in range(2):
        total = erecv[h * nr].astype(F32)
        for i in range(1, nr):
            total = total + erecv[h * nr + i].astype(F32)
        halves.append(total)
    ysend1[...] = screen(jnp.concatenate(halves, axis=1).astype(BF16))
    def cross(s, p):
        return remote(ysend1, yall1.at[me], last_send.at[0],
                      last_recv.at[r // 2 * 2 + plane], s, group * 2 + p)

    def hand(src, p):
        return remote(src, yall1.at[p], hand_send.at[0], hand_recv.at[0], mate, j)

    others = ([(s, p) for s in chips for p in (1 - plane, plane)] + [(r, 1 - plane)])
    for s, p in others:
        cross(s, p).start()
    hand(ysend1, me).start()
    yall1[me] = ysend1[...]
    arrived(kz0.at[1 - plane], mate_recv.at[0])
    energy = ec - evb[...]
    k0 = jnp.concatenate([kz0[h].astype(F32).T for h in range(2)], axis=0)
    out_ref[0] = energy * (energy * xv[0] + k0)
    swap.wait_send()
    sent(erecv.at[pl.ds(0, np - 1)], peer_send.at[1])
    sources = ([(lax.rem(r + nr - 2 * k, nr), p) for k in range(1, nr // 2)
                for p in (1 - plane, plane)])
    for s, p in [(r, 1 - plane)] + sources:
        block = yall1.at[s * 2 + p]
        arrived(block, last_recv.at[s // 2 * 2 + p])
        hand(block, s * 2 + p).start()
    arrived(yall1.at[pl.ds(0, nr)], hand_recv.at[0])
    k1t = jnp.dot(condt[...], yall1[...].reshape(np * nk, nv), preferred_element_type=F32)
    out_ref[0] += k1t.T
    sent(yall1.at[pl.ds(0, nr - 1)], last_send.at[0])
    sent(yall1.at[pl.ds(0, nr)], hand_send.at[0])


def fused(nr, nj, trial, screened, val_points, cond_points, eps_val, eps_cond):
    mb, nv = val_points.shape
    nb, cw = cond_points.shape
    np = 2 * nr
    nq = np // nj
    nk = nb // nq
    vh = nv // 2
    ng = nj // 2
    scratch = [
        pltpu.VMEM(trial.shape, F32),
        pltpu.VMEM(screened.shape, BF16),
        pltpu.VMEM((nq, nk, cw), BF16),
        pltpu.VMEM((1, nv), F32),
        pltpu.VMEM((1, eps_cond.shape[0]), F32),
        pltpu.VMEM((nr, LANES, nv), BF16),
        pltpu.VMEM((nq, nk, LANES), BF16),
        pltpu.VMEM((nr, nk, LANES), BF16),
        pltpu.VMEM((nq, nk, nv), BF16),
        pltpu.VMEM((nr, nk, nv), BF16),
        pltpu.VMEM((nq, nj, nk, cw), BF16),
        pltpu.VMEM((nv, LANES), F32),
        pltpu.VMEM((2, nk, vh), BF16),
        pltpu.VMEM((nk, nv), BF16),
        pltpu.VMEM((np, nk, vh), BF16),
        pltpu.VMEM((np, nk, nv), BF16),
        pltpu.VMEM((np, nk, vh), BF16),
        pltpu.VMEM((np, nk, vh), BF16),
        pltpu.VMEM((2, cw, vh), BF16),
        pltpu.VMEM((nk, nv), BF16),
        pltpu.VMEM((cw, vh), F32),
        pltpu.VMEM((cw, np * nk), BF16),
        pltpu.SemaphoreType.DMA((7,)),
        pltpu.SemaphoreType.DMA((2,)),
        pltpu.SemaphoreType.DMA((2,)),
        pltpu.SemaphoreType.DMA((1,)),
        pltpu.SemaphoreType.DMA((1,)),
        pltpu.SemaphoreType.DMA((2,)),
        pltpu.SemaphoreType.DMA((2,)),
        pltpu.SemaphoreType.DMA((1,)),
        pltpu.SemaphoreType.DMA((1,)),
        pltpu.SemaphoreType.DMA((1,)),
        pltpu.SemaphoreType.DMA((1,)),
        pltpu.SemaphoreType.DMA((nr // 2,)),
        pltpu.SemaphoreType.DMA((nr // 2,)),
        pltpu.SemaphoreType.DMA((1,)),
        pltpu.SemaphoreType.DMA((1,)),
        pltpu.SemaphoreType.DMA((1,)),
        pltpu.SemaphoreType.DMA((nr,)),
        pltpu.SemaphoreType.DMA((1,)),
        pltpu.SemaphoreType.DMA((1,)),
    ]
    return pl.pallas_call(
        functools.partial(kernel, nr, nj),
        out_shape=pltpu.VMEM(trial.shape, F32),
        in_specs=[pl.BlockSpec(memory_space=pltpu.HBM)] * 6,
        out_specs=pl.BlockSpec(memory_space=pltpu.VMEM),
        scratch_shapes=scratch,
        compiler_params=pltpu.CompilerParams(
            collective_id=0, has_side_effects=True, vmem_limit_bytes=64 * 2**20 - 2**18),
    )(trial, screened, val_points, cond_points.reshape(nq, nk, cw), eps_val[None], eps_cond[None])


def fits(nr, nj, trial, val_points, cond_points):
    mb, nv = val_points.shape
    nb, cw = cond_points.shape
    if nr % 2 or nj % 2 or (2 * nr) % nj or nb % (2 * nr // nj):
        return False
    nk = nb // (2 * nr // nj)
    return (trial.shape[0] == 1 and cw == LANES and nk % ROWS16 == 0
            and mb % ROWS16 == 0 and mb <= LANES and nv == 2 * LANES)


def general(trial, screened, val_points, cond_points, eps_val, eps_cond):
    cond_full = lax.all_gather(cond_points, "row", axis=1, tiled=True)
    energy_full = eps_cond[None, :] - eps_val[:, None]
    width = trial.shape[2]
    offset = lax.axis_index("row") * width
    x_full = lax.all_gather(trial.astype(BF16), "row", axis=2, tiled=True).astype(trial.dtype)
    xb_full = x_full.astype(BF16)
    x_mine = trial
    for step in range(APPLY):
        pair = jnp.einsum(
            "mv,bvc->bmc", val_points, xb_full, preferred_element_type=F32).astype(BF16)
        inner = jnp.einsum("bmc,nc->bmn", pair, cond_full, preferred_element_type=F32)
        tile = (screened[None] * inner).astype(BF16)
        back = jnp.einsum("bmn,nc->bmc", tile, cond_full, preferred_element_type=F32).astype(BF16)
        part_low = jnp.einsum(
            "mv,bmc->bvc", val_points, back, preferred_element_type=F32).astype(BF16)
        partial_terms = lax.optimization_barrier(part_low).astype(F32)
        kernel_full = lax.psum(partial_terms, ("row", "col"))
        x_full = energy_full[None] * x_full + kernel_full
        xb_full = x_full.astype(BF16)
        x_mine = lax.dynamic_slice_in_dim(x_full, offset, width, 2)
    return x_mine


def solution(mesh):
    nr, nj = mesh.shape["row"], mesh.shape["col"]

    def body(trial, screened, val_points, cond_points, eps_val, eps_cond):
        args = (trial, screened, val_points, cond_points, eps_val, eps_cond)
        if fits(nr, nj, trial, val_points, cond_points):
            return fused(nr, nj, *args)
        return general(*args)

    in_specs = (P(None, None, "row"), P("row", "col"), P("row", None), P("col", "row"), P(), P())
    out_specs = P(None, None, "row")
    return jax.shard_map(body, mesh=mesh, in_specs=in_specs, out_specs=out_specs, check_vma=False)
```

```python
import functools

import jax
import jax.numpy as jnp
from jax import lax
from jax.experimental import pallas as pl
from jax.experimental.pallas import tpu as pltpu
from jax.sharding import PartitionSpec as P

APPLY = 2
LANES = 128
ROWS16 = 16
F32 = jnp.float32
BF16 = jnp.bfloat16
MESH = pl.DeviceIdType.MESH


def dot_nt(a, b):
    return lax.dot_general(a, b, (((1,), (1,)), ((), ())), preferred_element_type=F32)


def kernel(nr, nj, x_hbm, s_hbm, v_hbm, c_hbm, ev_hbm, ec_hbm, out_ref,
           xv, sv, cv, evv, ecv, vall, st, sall, asend, arecv, call, evb,
           ysend0, ysend1, yall0, yall1, esend, erecv, kz0, w0, b1t, condt,
           local_sem, own_send, own_recv, col_send, col_recv, peer_send, peer_recv,
           mate_send, mate_recv, far_send, far_recv,
           val_send, val_recv, pass_send, pass_recv,
           last_send, last_recv, hand_send, hand_recv):
    r = lax.axis_index("row")
    j = lax.axis_index("col")
    group, plane = j // 2, lax.rem(j, 2)
    me = r * 2 + plane
    np = nr * 2
    nq = np // nj
    nh = nr // 2
    core = lax.rem(r, 2)

    def row_at(s):
        return lax.rem(s, 2) * nh + s // 2

    def peer_at(p):
        return lax.rem(p // 2, 2) * nr + p // 4 * 2 + lax.rem(p, 2)

    here_at = peer_at(me)
    mb, nv = v_hbm.shape
    _, nk, cw = c_hbm.shape
    nb = nq * nk
    vh = nv // 2

    loads = {}

    def load(names):
        for name, src, dst in names:
            loads[name] = pltpu.make_async_copy(src, dst, local_sem.at[len(loads)])
            loads[name].start()

    load([("c", c_hbm, cv), ("x", x_hbm, xv)])
    barrier = pltpu.get_barrier_semaphore()
    steps = sorted(range(1, np), key=lambda k: abs(k - np // 2))
    peers = [lax.rem(me + k, np) for k in steps]
    chips = [lax.rem(r + 2 * k, nr) for k in range(1, nr // 2)]
    mate = r + 1 - 2 * lax.rem(r, 2)
    col_peers = [lax.rem(j + k, nj) for k in range(1, nj)]
    far_groups = [lax.rem(group + k, nj // 2) for k in range(1, nj // 2)]
    for g in far_groups:
        for s in range(nr):
            pl.semaphore_signal(barrier, inc=1, device_id=(s, g * 2 + plane),
                                device_id_type=MESH)
        pl.semaphore_signal(barrier, inc=1, device_id=(r, g * 2 + 1 - plane),
                            device_id_type=MESH)
    for p in peers:
        pl.semaphore_signal(barrier, inc=1, device_id=(p // 2, group * 2 + lax.rem(p, 2)),
                            device_id_type=MESH)
    greeted = np - 1 + (nj // 2 - 1) * (nr + 1)

    load([("v", v_hbm, vall.at[row_at(r), pl.ds(0, mb)]), ("s", s_hbm, sv), ("ev", ev_hbm, evv),
          ("ec", ec_hbm, ecv), ("call", c_hbm, call.at[j // 2, :, lax.rem(j, 2)])])

    def remote(src, dst, send_sem, recv_sem, row, col):
        return pltpu.make_async_remote_copy(
            src_ref=src, dst_ref=dst, send_sem=send_sem, recv_sem=recv_sem,
            device_id=(row, col), device_id_type=MESH)

    def arrived(ref, sem):
        remote(ref, ref, col_send.at[0], sem, mate, j).wait_recv()

    def sent(ref, sem):
        remote(ref, ref, sem, col_recv.at[0], mate, j).wait_send()

    def val_block(s):
        return vall.at[row_at(s), pl.ds(0, mb)]

    def val_copy(s):
        return remote(v_hbm, val_block(r), val_send.at[s // 2], val_recv.at[r // 2], s, j)

    def pass_copy(s):
        return remote(val_block(s), val_block(s), pass_send.at[0], pass_recv.at[0], mate, j)

    def peer_copy(phase, src, dst, peer):
        return remote(src, dst, peer_send.at[phase], peer_recv.at[phase],
                      peer // 2, group * 2 + lax.rem(peer, 2))

    def owner_copy(phase, src, dst, q, g):
        return remote(src, dst, own_send.at[phase], own_recv.at[phase],
                      q * (nj // 2) + group, g * 2 + plane)

    groups = [lax.rem(group + k, nj // 2) for k in range(nj // 2)]

    def owner_each(q, g, away, here):
        if g is groups[0]:
            itself = q * (nj // 2) + group == r
            pl.when(jnp.logical_not(itself))(away)
            if here is not None:
                pl.when(itself)(here)
        else:
            away()

    def owner_send(phase, buffer, target, slot, chosen):
        for g in chosen:
            for q in range(nq):
                def away():
                    owner_copy(phase, buffer.at[q], target.at[slot], q, g).start()

                def here():
                    target[slot] = buffer[q]

                owner_each(q, g, away, here)

    holder = lax.rem(r, nj // 2) * 2 + plane
    holds = holder == j

    def far_copy(g):
        return remote(w0, w0, far_send.at[0], far_recv.at[0], r, g * 2 + plane)

    def all_send(phase, src_of, dst):
        for p in peers:
            peer_copy(phase, src_of(p), dst, p).start()

    loads["c"].wait()
    loads["x"].wait()
    first = dot_nt(cv[...].reshape(nb, cw), xv[0].astype(BF16))
    asend[...] = first.astype(BF16).reshape(asend.shape)

    pl.semaphore_wait(barrier, greeted)
    owner_send(0, asend, arecv, r, groups[:1])
    for s in chips:
        val_copy(s).start()
    loads["v"].wait()
    pass_copy(r).start()

    loads["s"].wait()
    scr = sv[...].astype(F32)
    scr = jnp.concatenate([scr, jnp.zeros((LANES - mb, nb), F32)], axis=0)
    wide = -(-nb // LANES) * LANES
    if wide > nb:
        scr = jnp.concatenate([scr, jnp.zeros((LANES, wide - nb), F32)], axis=1)
    scr = scr.T
    st[...] = scr[:nb].astype(BF16).reshape(st.shape)
    owner_send(1, st, sall, row_at(r), groups[1:] + groups[:1])
    for s in col_peers:
        remote(c_hbm, call.at[j // 2, :, lax.rem(j, 2)], col_send.at[0], col_recv.at[0], r, s).start()

    if mb < LANES:
        for i in range(nr):
            vall[i, pl.ds(mb, LANES - mb)] = jnp.zeros((LANES - mb, nv), BF16)
    for name in ("ev", "ec", "call"):
        loads[name].wait()
    evb[...] = jnp.broadcast_to(evv[...], (LANES, nv)).T
    ec = ecv[:, pl.ds(pl.multiple_of(r * cw, cw), cw)]

    def screen_half(w, h):
        allv = vall[pl.ds(h * nh, nh)].reshape(nh * LANES, nv)
        inner = dot_nt(w, allv)
        tile = jnp.concatenate(
            [(sall[h * nh + i].astype(F32) * inner[:, i * LANES:(i + 1) * LANES]).astype(BF16)
             for i in range(nh)], axis=1)
        return jnp.dot(tile, allv, preferred_element_type=F32)

    mine = pl.ds(pl.multiple_of(plane * vh, vh), vh)
    b1t[...] = ((ec - evb[mine, :]) * xv[0, mine, :]).T

    @pl.when(holds)
    def _():
        arrived(arecv.at[pl.ds(0, nr - 1)], own_recv.at[0])
        total = arecv[0].astype(F32)
        for i in range(1, nr):
            total = total + arecv[i].astype(F32)
        w0[...] = total.astype(BF16)
        for g in groups[1:]:
            far_copy(g).start()

    for s in reversed(chips):
        arrived(val_block(s), val_recv.at[s // 2])
        pass_copy(s).start()

    @pl.when(holds)
    def _():
        arrived(sall.at[pl.ds(0, nr - 1)], own_recv.at[1])

    @pl.when(jnp.logical_not(holds))
    def _():
        arrived(sall, own_recv.at[1])
        arrived(w0, far_recv.at[0])

    w = w0[...]
    y0 = screen_half(w, core)
    arrived(vall.at[pl.ds(0, nh), pl.ds(0, mb)], pass_recv.at[0])
    y0 = (y0 + screen_half(w, 1 - core)).astype(BF16)
    ysend0[0] = y0[:, :vh]
    ysend0[1] = y0[:, vh:]
    all_send(0, lambda p: ysend0.at[lax.rem(p, 2)], yall0.at[here_at])
    yall0[here_at] = ysend0[plane]
    arrived(esend.at[pl.ds(0, nq * (nj - 1))], col_recv.at[0])
    condt[...] = call[...].reshape(np * nk, cw).T
    for s in chips:
        val_copy(s).wait_send()
    sent(vall.at[pl.ds(0, nr // 2), pl.ds(0, mb)], pass_send.at[0])
    sent(esend.at[pl.ds(0, nq * (nj - 1))], col_send.at[0])

    @pl.when(holds)
    def _():
        sent(asend.at[pl.ds(0, nq - 1)], own_send.at[0])
        sent(sall.at[pl.ds(0, nr - 1)], own_send.at[1])
        sent(arecv.at[pl.ds(0, nj // 2 - 1)], far_send.at[0])

    @pl.when(jnp.logical_not(holds))
    def _():
        sent(asend, own_send.at[0])
        sent(sall, own_send.at[1])

    arrived(yall0.at[pl.ds(0, np - 1)], peer_recv.at[0])
    k0t = jnp.dot(condt[...], yall0[...].reshape(np * nk, vh), preferred_element_type=F32)
    x1t = (b1t[...] + k0t).astype(BF16)

    cond = call[...].reshape(np * nk, cw)
    esend[...] = jnp.dot(cond, x1t, preferred_element_type=F32).astype(BF16).reshape(esend.shape)
    all_send(1, lambda p: esend.at[peer_at(p)], erecv.at[plane * nr + r])
    erecv[plane * nr + r] = esend[here_at]
    kz0[plane] = k0t.astype(BF16)

    other = group * 2 + 1 - plane
    swap = remote(kz0.at[plane], kz0.at[plane], mate_send.at[0], mate_recv.at[0], r, other)
    swap.start()
    sent(yall0.at[pl.ds(0, np - 1)], peer_send.at[0])
    arrived(erecv.at[pl.ds(0, np - 1)], peer_recv.at[1])

    halves = []
    for h in range(2):
        total = erecv[h * nr].astype(F32)
        for i in range(1, nr):
            total = total + erecv[h * nr + i].astype(F32)
        halves.append(total)
    w = jnp.concatenate(halves, axis=1).astype(BF16)
    ysend1[...] = (screen_half(w, core) + screen_half(w, 1 - core)).astype(BF16)
    def cross(s, p):
        return remote(ysend1, yall1.at[here_at], last_send.at[0],
                      last_recv.at[r // 2 * 2 + plane], s, group * 2 + p)

    def hand(src, p):
        return remote(src, yall1.at[peer_at(p)], hand_send.at[0], hand_recv.at[0], mate, j)

    others = ([(s, p) for s in chips for p in (1 - plane, plane)] + [(r, 1 - plane)])
    for s, p in others:
        cross(s, p).start()
    hand(ysend1, me).start()
    yall1[here_at] = ysend1[...]
    arrived(kz0.at[1 - plane], mate_recv.at[0])
    energy = ec - evb[...]
    k0 = jnp.concatenate([kz0[h].astype(F32).T for h in range(2)], axis=0)
    out_ref[0] = energy * (energy * xv[0] + k0)
    swap.wait_send()
    sent(erecv.at[pl.ds(0, np - 1)], peer_send.at[1])
    sources = ([(lax.rem(r + nr - 2 * k, nr), p) for k in range(1, nr // 2)
                for p in (1 - plane, plane)])
    for s, p in [(r, 1 - plane)] + sources:
        block = yall1.at[peer_at(s * 2 + p)]
        arrived(block, last_recv.at[s // 2 * 2 + p])
        hand(block, s * 2 + p).start()

    def last_half(h):
        columns = pl.ds(pl.multiple_of(h * (nr * nk), LANES), nr * nk)
        blocks = yall1[pl.ds(h * nr, nr)].reshape(nr * nk, nv)
        return jnp.dot(condt[:, columns], blocks, preferred_element_type=F32).T

    out_ref[0] += last_half(core)
    arrived(yall1.at[pl.ds(0, nr)], hand_recv.at[0])
    out_ref[0] += last_half(1 - core)
    sent(yall1.at[pl.ds(0, nr - 1)], last_send.at[0])
    sent(yall1.at[pl.ds(0, nr)], hand_send.at[0])


def fused(nr, nj, trial, screened, val_points, cond_points, eps_val, eps_cond):
    mb, nv = val_points.shape
    nb, cw = cond_points.shape
    np = 2 * nr
    nq = np // nj
    nk = nb // nq
    vh = nv // 2
    ng = nj // 2
    scratch = [
        pltpu.VMEM(trial.shape, F32),
        pltpu.VMEM(screened.shape, BF16),
        pltpu.VMEM((nq, nk, cw), BF16),
        pltpu.VMEM((1, nv), F32),
        pltpu.VMEM((1, eps_cond.shape[0]), F32),
        pltpu.VMEM((nr, LANES, nv), BF16),
        pltpu.VMEM((nq, nk, LANES), BF16),
        pltpu.VMEM((nr, nk, LANES), BF16),
        pltpu.VMEM((nq, nk, nv), BF16),
        pltpu.VMEM((nr, nk, nv), BF16),
        pltpu.VMEM((ng, nq, 2, nk, cw), BF16),
        pltpu.VMEM((nv, LANES), F32),
        pltpu.VMEM((2, nk, vh), BF16),
        pltpu.VMEM((nk, nv), BF16),
        pltpu.VMEM((np, nk, vh), BF16),
        pltpu.VMEM((np, nk, nv), BF16),
        pltpu.VMEM((np, nk, vh), BF16),
        pltpu.VMEM((np, nk, vh), BF16),
        pltpu.VMEM((2, cw, vh), BF16),
        pltpu.VMEM((nk, nv), BF16),
        pltpu.VMEM((cw, vh), F32),
        pltpu.VMEM((cw, np * nk), BF16),
        pltpu.SemaphoreType.DMA((7,)),
        pltpu.SemaphoreType.DMA((2,)),
        pltpu.SemaphoreType.DMA((2,)),
        pltpu.SemaphoreType.DMA((1,)),
        pltpu.SemaphoreType.DMA((1,)),
        pltpu.SemaphoreType.DMA((2,)),
        pltpu.SemaphoreType.DMA((2,)),
        pltpu.SemaphoreType.DMA((1,)),
        pltpu.SemaphoreType.DMA((1,)),
        pltpu.SemaphoreType.DMA((1,)),
        pltpu.SemaphoreType.DMA((1,)),
        pltpu.SemaphoreType.DMA((nr // 2,)),
        pltpu.SemaphoreType.DMA((nr // 2,)),
        pltpu.SemaphoreType.DMA((1,)),
        pltpu.SemaphoreType.DMA((1,)),
        pltpu.SemaphoreType.DMA((1,)),
        pltpu.SemaphoreType.DMA((nr,)),
        pltpu.SemaphoreType.DMA((1,)),
        pltpu.SemaphoreType.DMA((1,)),
    ]
    return pl.pallas_call(
        functools.partial(kernel, nr, nj),
        out_shape=pltpu.VMEM(trial.shape, F32),
        in_specs=[pl.BlockSpec(memory_space=pltpu.HBM)] * 6,
        out_specs=pl.BlockSpec(memory_space=pltpu.VMEM),
        scratch_shapes=scratch,
        compiler_params=pltpu.CompilerParams(
            collective_id=0, has_side_effects=True, vmem_limit_bytes=64 * 2**20 - 2**18),
    )(trial, screened, val_points, cond_points.reshape(nq, nk, cw), eps_val[None], eps_cond[None])


def fits(nr, nj, trial, val_points, cond_points):
    mb, nv = val_points.shape
    nb, cw = cond_points.shape
    if nr % 2 or nj % 2 or (2 * nr) % nj or nb % (2 * nr // nj):
        return False
    nk = nb // (2 * nr // nj)
    return (trial.shape[0] == 1 and cw == LANES and nk % ROWS16 == 0
            and mb % ROWS16 == 0 and mb <= LANES and nv == 2 * LANES
            and nj // 2 == 2 and nr * nk % LANES == 0)


def general(trial, screened, val_points, cond_points, eps_val, eps_cond):
    cond_full = lax.all_gather(cond_points, "row", axis=1, tiled=True)
    energy_full = eps_cond[None, :] - eps_val[:, None]
    width = trial.shape[2]
    offset = lax.axis_index("row") * width
    x_full = lax.all_gather(trial.astype(BF16), "row", axis=2, tiled=True).astype(trial.dtype)
    xb_full = x_full.astype(BF16)
    x_mine = trial
    for step in range(APPLY):
        pair = jnp.einsum(
            "mv,bvc->bmc", val_points, xb_full, preferred_element_type=F32).astype(BF16)
        inner = jnp.einsum("bmc,nc->bmn", pair, cond_full, preferred_element_type=F32)
        tile = (screened[None] * inner).astype(BF16)
        back = jnp.einsum("bmn,nc->bmc", tile, cond_full, preferred_element_type=F32).astype(BF16)
        part_low = jnp.einsum(
            "mv,bmc->bvc", val_points, back, preferred_element_type=F32).astype(BF16)
        partial_terms = lax.optimization_barrier(part_low).astype(F32)
        kernel_full = lax.psum(partial_terms, ("row", "col"))
        x_full = energy_full[None] * x_full + kernel_full
        xb_full = x_full.astype(BF16)
        x_mine = lax.dynamic_slice_in_dim(x_full, offset, width, 2)
    return x_mine


def solution(mesh):
    nr, nj = mesh.shape["row"], mesh.shape["col"]

    def body(trial, screened, val_points, cond_points, eps_val, eps_cond):
        args = (trial, screened, val_points, cond_points, eps_val, eps_cond)
        if fits(nr, nj, trial, val_points, cond_points):
            return fused(nr, nj, *args)
        return general(*args)

    in_specs = (P(None, None, "row"), P("row", "col"), P("row", None), P("col", "row"), P(), P())
    out_specs = P(None, None, "row")
    return jax.shard_map(body, mesh=mesh, in_specs=in_specs, out_specs=out_specs, check_vma=False)
```

```python
import functools

import jax
import jax.numpy as jnp
from jax import lax
from jax.experimental import pallas as pl
from jax.experimental.pallas import tpu as pltpu
from jax.sharding import PartitionSpec as P

APPLY = 2
LANES = 128
ROWS16 = 16
F32 = jnp.float32
BF16 = jnp.bfloat16
MESH = pl.DeviceIdType.MESH


def dot_nt(a, b):
    return lax.dot_general(a, b, (((1,), (1,)), ((), ())), preferred_element_type=F32)


def wrap(x, n):
    return lax.select(x >= n, x - n, x)


def kernel(nr, nj, x_hbm, s_hbm, v_hbm, c_hbm, ev_hbm, ec_hbm, out_ref,
           xv, sv, cv, evv, ecv, vall, st, sall, asend, arecv, call, evb,
           ysend0, ysend1, yall0, yall1, esend, erecv, kz0, w0, b1t, condt,
           local_sem, own_send, own_recv, col_send, col_recv, peer_send, peer_recv,
           mate_send, mate_recv, far_send, far_recv,
           val_send, val_recv, pass_send, pass_recv,
           last_send, last_recv, hand_send, hand_recv):
    r = lax.axis_index("row")
    j = lax.axis_index("col")
    group, plane = j // 2, lax.rem(j, 2)
    me = r * 2 + plane
    np = nr * 2
    nq = np // nj
    mb, nv = v_hbm.shape
    _, nk, cw = c_hbm.shape
    nb = nq * nk
    vh = nv // 2

    loads = {}

    def load(names):
        for name, src, dst in names:
            loads[name] = pltpu.make_async_copy(src, dst, local_sem.at[len(loads)])
            loads[name].start()

    load([("c", c_hbm, cv), ("x", x_hbm, xv)])
    barrier = pltpu.get_barrier_semaphore()
    across = group * 2 + 1 - plane
    planes = [(1 - plane, across), (plane, j)]
    row_steps = sorted(range(nr), key=lambda k: abs(k - nr // 2))
    rows = {k: wrap(r + k, nr) if k else r for k in range(nr)}
    peers = [(rows[k], p, col) for k in row_steps for p, col in planes if k or col is across]
    chips = [rows[2 * k] for k in range(1, nr // 2)]
    mate = r + 1 - 2 * lax.rem(r, 2)
    col_peers = [wrap(j + k, nj) for k in range(1, nj)]
    far_groups = [wrap(group + k, nj // 2) for k in range(1, nj // 2)]
    for g in far_groups:
        for s in range(nr):
            pl.semaphore_signal(barrier, inc=1, device_id=(s, g * 2 + plane),
                                device_id_type=MESH)
        pl.semaphore_signal(barrier, inc=1, device_id=(r, g * 2 + 1 - plane),
                            device_id_type=MESH)
    for s, p, col in peers:
        pl.semaphore_signal(barrier, inc=1, device_id=(s, col), device_id_type=MESH)
    greeted = np - 1 + (nj // 2 - 1) * (nr + 1)

    load([("v", v_hbm, vall.at[r, pl.ds(0, mb)]), ("s", s_hbm, sv), ("ev", ev_hbm, evv),
          ("ec", ec_hbm, ecv), ("call", c_hbm, call.at[:, j])])

    def remote(src, dst, send_sem, recv_sem, row, col):
        return pltpu.make_async_remote_copy(
            src_ref=src, dst_ref=dst, send_sem=send_sem, recv_sem=recv_sem,
            device_id=(row, col), device_id_type=MESH)

    def arrived(ref, sem):
        remote(ref, ref, col_send.at[0], sem, mate, j).wait_recv()

    def sent(ref, sem):
        remote(ref, ref, sem, col_recv.at[0], mate, j).wait_send()

    def val_block(s):
        return vall.at[s, pl.ds(0, mb)]

    def val_copy(s):
        return remote(v_hbm, val_block(r), val_send.at[s // 2], val_recv.at[r // 2], s, j)

    def pass_copy(s):
        return remote(val_block(s), val_block(s), pass_send.at[0], pass_recv.at[0], mate, j)

    def owner_copy(phase, src, dst, q, g):
        return remote(src, dst, own_send.at[phase], own_recv.at[phase],
                      q * (nj // 2) + group, g * 2 + plane)

    groups = [group] + far_groups

    def owner_each(q, g, away, here):
        if g is groups[0]:
            itself = q * (nj // 2) + group == r
            pl.when(jnp.logical_not(itself))(away)
            if here is not None:
                pl.when(itself)(here)
        else:
            away()

    def owner_send(phase, buffer, target, chosen):
        for g in chosen:
            for q in range(nq):
                def away():
                    owner_copy(phase, buffer.at[q], target.at[r], q, g).start()

                def here():
                    target[r] = buffer[q]

                owner_each(q, g, away, here)

    holder = lax.rem(r, nj // 2) * 2 + plane
    holds = holder == j

    def far_copy(g):
        return remote(w0, w0, far_send.at[0], far_recv.at[0], r, g * 2 + plane)

    def all_send(phase, src_of, dst):
        for s, p, col in peers:
            remote(src_of(s, p), dst, peer_send.at[phase], peer_recv.at[phase], s, col).start()

    loads["c"].wait()
    loads["x"].wait()
    first = dot_nt(cv[...].reshape(nb, cw), xv[0].astype(BF16))
    asend[...] = first.astype(BF16).reshape(asend.shape)

    pl.semaphore_wait(barrier, greeted)
    owner_send(0, asend, arecv, groups[:1])
    for s in chips:
        val_copy(s).start()
    loads["v"].wait()
    pass_copy(r).start()

    loads["s"].wait()
    scr = sv[...].astype(F32)
    scr = jnp.concatenate([scr, jnp.zeros((LANES - mb, nb), F32)], axis=0)
    wide = -(-nb // LANES) * LANES
    if wide > nb:
        scr = jnp.concatenate([scr, jnp.zeros((LANES, wide - nb), F32)], axis=1)
    scr = scr.T
    st[...] = scr[:nb].astype(BF16).reshape(st.shape)
    owner_send(1, st, sall, groups[1:] + groups[:1])
    for s in col_peers:
        remote(c_hbm, call.at[:, j], col_send.at[0], col_recv.at[0], r, s).start()

    if mb < LANES:
        for i in range(nr):
            vall[i, pl.ds(mb, LANES - mb)] = jnp.zeros((LANES - mb, nv), BF16)
    for name in ("ev", "ec", "call"):
        loads[name].wait()
    evb[...] = jnp.broadcast_to(evv[...], (LANES, nv)).T
    ec = ecv[:, pl.ds(pl.multiple_of(r * cw, cw), cw)]

    def screen(w):
        allv = vall[...].reshape(nr * LANES, nv)
        inner = dot_nt(w, allv)
        tile = jnp.concatenate(
            [(sall[i].astype(F32) * inner[:, i * LANES:(i + 1) * LANES]).astype(BF16)
             for i in range(nr)], axis=1)
        return jnp.dot(tile, allv, preferred_element_type=F32).astype(BF16)

    mine = pl.ds(pl.multiple_of(plane * vh, vh), vh)
    b1t[...] = ((ec - evb[mine, :]) * xv[0, mine, :]).T

    @pl.when(holds)
    def _():
        arrived(arecv.at[pl.ds(0, nr - 1)], own_recv.at[0])
        total = arecv[0].astype(F32)
        for i in range(1, nr):
            total = total + arecv[i].astype(F32)
        w0[...] = total.astype(BF16)
        for g in groups[1:]:
            far_copy(g).start()

    for s in reversed(chips):
        arrived(val_block(s), val_recv.at[s // 2])
        pass_copy(s).start()

    @pl.when(holds)
    def _():
        arrived(sall.at[pl.ds(0, nr - 1)], own_recv.at[1])

    @pl.when(jnp.logical_not(holds))
    def _():
        arrived(sall, own_recv.at[1])
        arrived(w0, far_recv.at[0])

    arrived(vall.at[pl.ds(0, nr // 2), pl.ds(0, mb)], pass_recv.at[0])
    y0 = screen(w0[...])
    ysend0[0] = y0[:, :vh]
    ysend0[1] = y0[:, vh:]
    all_send(0, lambda s, p: ysend0.at[p], yall0.at[me])
    yall0[me] = ysend0[plane]
    arrived(call.at[:, pl.ds(0, nj - 1)], col_recv.at[0])
    condt[...] = call[...].reshape(np * nk, cw).T
    for s in chips:
        val_copy(s).wait_send()
    sent(vall.at[pl.ds(0, nr // 2), pl.ds(0, mb)], pass_send.at[0])
    sent(call.at[:, pl.ds(0, nj - 1)], col_send.at[0])

    @pl.when(holds)
    def _():
        sent(asend.at[pl.ds(0, nq - 1)], own_send.at[0])
        sent(sall.at[pl.ds(0, nr - 1)], own_send.at[1])
        sent(arecv.at[pl.ds(0, nj // 2 - 1)], far_send.at[0])

    @pl.when(jnp.logical_not(holds))
    def _():
        sent(asend, own_send.at[0])
        sent(sall, own_send.at[1])

    arrived(yall0.at[pl.ds(0, np - 1)], peer_recv.at[0])
    k0t = jnp.dot(condt[...], yall0[...].reshape(np * nk, vh), preferred_element_type=F32)
    x1t = (b1t[...] + k0t).astype(BF16)

    cond = call[...].reshape(np * nk, cw)
    esend[...] = jnp.dot(cond, x1t, preferred_element_type=F32).astype(BF16).reshape(esend.shape)
    all_send(1, lambda s, p: esend.at[s * 2 + p], erecv.at[plane * nr + r])
    erecv[plane * nr + r] = esend[me]
    kz0[plane] = k0t.astype(BF16)

    swap = remote(kz0.at[plane], kz0.at[plane], mate_send.at[0], mate_recv.at[0], r, across)
    swap.start()
    sent(yall0.at[pl.ds(0, np - 1)], peer_send.at[0])
    arrived(erecv.at[pl.ds(0, np - 1)], peer_recv.at[1])

    halves = []
    for h in range(2):
        total = erecv[h * nr].astype(F32)
        for i in range(1, nr):
            total = total + erecv[h * nr + i].astype(F32)
        halves.append(total)
    ysend1[...] = screen(jnp.concatenate(halves, axis=1).astype(BF16))
    from_slot = last_recv.at[r // 2 * 2 + plane]

    def cross(s, col):
        return remote(ysend1, yall1.at[me], last_send.at[0], from_slot, s, col)

    def hand(src, p):
        return remote(src, yall1.at[p], hand_send.at[0], hand_recv.at[0], mate, j)

    for s in chips:
        for p, col in planes:
            cross(s, col).start()
    cross(r, across).start()
    hand(ysend1, me).start()
    yall1[me] = ysend1[...]
    arrived(kz0.at[1 - plane], mate_recv.at[0])
    energy = ec - evb[...]
    k0 = jnp.concatenate([kz0[h].astype(F32).T for h in range(2)], axis=0)
    out_ref[0] = energy * (energy * xv[0] + k0)
    swap.wait_send()
    sent(erecv.at[pl.ds(0, np - 1)], peer_send.at[1])
    sources = ([(rows[nr - 2 * k], p) for k in range(1, nr // 2)
                for p in (1 - plane, plane)])
    for s, p in [(r, 1 - plane)] + sources:
        block = yall1.at[s * 2 + p]
        arrived(block, last_recv.at[s // 2 * 2 + p])
        hand(block, s * 2 + p).start()
    arrived(yall1.at[pl.ds(0, nr)], hand_recv.at[0])
    k1t = jnp.dot(condt[...], yall1[...].reshape(np * nk, nv), preferred_element_type=F32)
    out_ref[0] += k1t.T
    sent(yall1.at[pl.ds(0, nr - 1)], last_send.at[0])
    sent(yall1.at[pl.ds(0, nr)], hand_send.at[0])


def fused(nr, nj, trial, screened, val_points, cond_points, eps_val, eps_cond):
    mb, nv = val_points.shape
    nb, cw = cond_points.shape
    np = 2 * nr
    nq = np // nj
    nk = nb // nq
    vh = nv // 2
    ng = nj // 2
    scratch = [
        pltpu.VMEM(trial.shape, F32),
        pltpu.VMEM(screened.shape, BF16),
        pltpu.VMEM((nq, nk, cw), BF16),
        pltpu.VMEM((1, nv), F32),
        pltpu.VMEM((1, eps_cond.shape[0]), F32),
        pltpu.VMEM((nr, LANES, nv), BF16),
        pltpu.VMEM((nq, nk, LANES), BF16),
        pltpu.VMEM((nr, nk, LANES), BF16),
        pltpu.VMEM((nq, nk, nv), BF16),
        pltpu.VMEM((nr, nk, nv), BF16),
        pltpu.VMEM((nq, nj, nk, cw), BF16),
        pltpu.VMEM((nv, LANES), F32),
        pltpu.VMEM((2, nk, vh), BF16),
        pltpu.VMEM((nk, nv), BF16),
        pltpu.VMEM((np, nk, vh), BF16),
        pltpu.VMEM((np, nk, nv), BF16),
        pltpu.VMEM((np, nk, vh), BF16),
        pltpu.VMEM((np, nk, vh), BF16),
        pltpu.VMEM((2, cw, vh), BF16),
        pltpu.VMEM((nk, nv), BF16),
        pltpu.VMEM((cw, vh), F32),
        pltpu.VMEM((cw, np * nk), BF16),
        pltpu.SemaphoreType.DMA((7,)),
        pltpu.SemaphoreType.DMA((2,)),
        pltpu.SemaphoreType.DMA((2,)),
        pltpu.SemaphoreType.DMA((1,)),
        pltpu.SemaphoreType.DMA((1,)),
        pltpu.SemaphoreType.DMA((2,)),
        pltpu.SemaphoreType.DMA((2,)),
        pltpu.SemaphoreType.DMA((1,)),
        pltpu.SemaphoreType.DMA((1,)),
        pltpu.SemaphoreType.DMA((1,)),
        pltpu.SemaphoreType.DMA((1,)),
        pltpu.SemaphoreType.DMA((nr // 2,)),
        pltpu.SemaphoreType.DMA((nr // 2,)),
        pltpu.SemaphoreType.DMA((1,)),
        pltpu.SemaphoreType.DMA((1,)),
        pltpu.SemaphoreType.DMA((1,)),
        pltpu.SemaphoreType.DMA((nr,)),
        pltpu.SemaphoreType.DMA((1,)),
        pltpu.SemaphoreType.DMA((1,)),
    ]
    return pl.pallas_call(
        functools.partial(kernel, nr, nj),
        out_shape=pltpu.VMEM(trial.shape, F32),
        in_specs=[pl.BlockSpec(memory_space=pltpu.HBM)] * 6,
        out_specs=pl.BlockSpec(memory_space=pltpu.VMEM),
        scratch_shapes=scratch,
        compiler_params=pltpu.CompilerParams(
            collective_id=0, has_side_effects=True, vmem_limit_bytes=64 * 2**20 - 2**18),
    )(trial, screened, val_points, cond_points.reshape(nq, nk, cw), eps_val[None], eps_cond[None])


def fits(nr, nj, trial, val_points, cond_points):
    mb, nv = val_points.shape
    nb, cw = cond_points.shape
    if nr % 2 or nj % 2 or (2 * nr) % nj or nb % (2 * nr // nj):
        return False
    nk = nb // (2 * nr // nj)
    return (trial.shape[0] == 1 and cw == LANES and nk % ROWS16 == 0
            and mb % ROWS16 == 0 and mb <= LANES and nv == 2 * LANES)


def general(trial, screened, val_points, cond_points, eps_val, eps_cond):
    cond_full = lax.all_gather(cond_points, "row", axis=1, tiled=True)
    energy_full = eps_cond[None, :] - eps_val[:, None]
    width = trial.shape[2]
    offset = lax.axis_index("row") * width
    x_full = lax.all_gather(trial.astype(BF16), "row", axis=2, tiled=True).astype(trial.dtype)
    xb_full = x_full.astype(BF16)
    x_mine = trial
    for step in range(APPLY):
        pair = jnp.einsum(
            "mv,bvc->bmc", val_points, xb_full, preferred_element_type=F32).astype(BF16)
        inner = jnp.einsum("bmc,nc->bmn", pair, cond_full, preferred_element_type=F32)
        tile = (screened[None] * inner).astype(BF16)
        back = jnp.einsum("bmn,nc->bmc", tile, cond_full, preferred_element_type=F32).astype(BF16)
        part_low = jnp.einsum(
            "mv,bmc->bvc", val_points, back, preferred_element_type=F32).astype(BF16)
        partial_terms = lax.optimization_barrier(part_low).astype(F32)
        kernel_full = lax.psum(partial_terms, ("row", "col"))
        x_full = energy_full[None] * x_full + kernel_full
        xb_full = x_full.astype(BF16)
        x_mine = lax.dynamic_slice_in_dim(x_full, offset, width, 2)
    return x_mine


def solution(mesh):
    nr, nj = mesh.shape["row"], mesh.shape["col"]

    def body(trial, screened, val_points, cond_points, eps_val, eps_cond):
        args = (trial, screened, val_points, cond_points, eps_val, eps_cond)
        if fits(nr, nj, trial, val_points, cond_points):
            return fused(nr, nj, *args)
        return general(*args)

    in_specs = (P(None, None, "row"), P("row", "col"), P("row", None), P("col", "row"), P(), P())
    out_specs = P(None, None, "row")
    return jax.shard_map(body, mesh=mesh, in_specs=in_specs, out_specs=out_specs, check_vma=False)
```

```python
import functools

import jax
import jax.numpy as jnp
from jax import lax
from jax.experimental import pallas as pl
from jax.experimental.pallas import tpu as pltpu
from jax.sharding import PartitionSpec as P

APPLY = 2
LANES = 128
ROWS16 = 16
F32 = jnp.float32
BF16 = jnp.bfloat16
MESH = pl.DeviceIdType.MESH


def dot_nt(a, b):
    return lax.dot_general(a, b, (((1,), (1,)), ((), ())), preferred_element_type=F32)


def wrap(x, n):
    return lax.select(x >= n, x - n, x)


def kernel(nr, nj, x_hbm, s_hbm, v_hbm, c_hbm, ev_hbm, ec_hbm, out_ref,
           xv, sv, cv, evv, ecv, vall, st, sall, asend, arecv, call, evb,
           ysend0, ysend1, yall0, yall1, esend, erecv, kz0, w0, b1t, condt,
           local_sem, own_send, own_recv, col_send, col_recv, peer_send, peer_recv,
           mate_send, mate_recv, far_send, far_recv,
           val_send, val_recv, pass_send, pass_recv,
           last_send, last_recv, hand_send, hand_recv):
    r = lax.axis_index("row")
    j = lax.axis_index("col")
    group, plane = j // 2, lax.rem(j, 2)
    me = r * 2 + plane
    np = nr * 2
    nq = np // nj
    mb, nv = v_hbm.shape
    _, nk, cw = c_hbm.shape
    nb = nq * nk
    vh = nv // 2

    loads = {}

    def load(names):
        for name, src, dst in names:
            loads[name] = pltpu.make_async_copy(src, dst, local_sem.at[len(loads)])
            loads[name].start()

    load([("c", c_hbm, cv), ("x", x_hbm, xv)])
    barrier = pltpu.get_barrier_semaphore()
    across = group * 2 + 1 - plane
    planes = [(1 - plane, across), (plane, j)]
    row_steps = sorted(range(nr), key=lambda k: abs(k - nr // 2))
    rows = {k: wrap(r + k, nr) if k else r for k in range(nr)}
    peers = [(rows[k], p, col) for k in row_steps for p, col in planes if k or col is across]
    chips = [rows[2 * k] for k in range(1, nr // 2)]
    mate = r + 1 - 2 * lax.rem(r, 2)
    col_peers = [wrap(j + k, nj) for k in range(1, nj)]
    far_groups = [wrap(group + k, nj // 2) for k in range(1, nj // 2)]
    for g in far_groups:
        for s in range(nr):
            pl.semaphore_signal(barrier, inc=1, device_id=(s, g * 2 + plane),
                                device_id_type=MESH)
        pl.semaphore_signal(barrier, inc=1, device_id=(r, g * 2 + 1 - plane),
                            device_id_type=MESH)
    for s, p, col in peers:
        pl.semaphore_signal(barrier, inc=1, device_id=(s, col), device_id_type=MESH)
    greeted = np - 1 + (nj // 2 - 1) * (nr + 1)

    load([("v", v_hbm, vall.at[r, pl.ds(0, mb)]), ("s", s_hbm, sv), ("ev", ev_hbm, evv),
          ("ec", ec_hbm, ecv), ("call", c_hbm, call.at[:, j])])

    def remote(src, dst, send_sem, recv_sem, row, col):
        return pltpu.make_async_remote_copy(
            src_ref=src, dst_ref=dst, send_sem=send_sem, recv_sem=recv_sem,
            device_id=(row, col), device_id_type=MESH)

    def arrived(ref, sem):
        remote(ref, ref, col_send.at[0], sem, mate, j).wait_recv()

    def sent(ref, sem):
        remote(ref, ref, sem, col_recv.at[0], mate, j).wait_send()

    def val_block(s):
        return vall.at[s, pl.ds(0, mb)]

    def val_copy(s):
        return remote(v_hbm, val_block(r), val_send.at[s // 2], val_recv.at[r // 2], s, j)

    def pass_copy(s):
        return remote(val_block(s), val_block(s), pass_send.at[0], pass_recv.at[0], mate, j)

    def owner_copy(phase, src, dst, q, g):
        return remote(src, dst, own_send.at[phase], own_recv.at[phase],
                      q * (nj // 2) + group, g * 2 + plane)

    groups = [group] + far_groups

    def owner_each(q, g, away, here):
        if g is groups[0]:
            itself = q * (nj // 2) + group == r
            pl.when(jnp.logical_not(itself))(away)
            if here is not None:
                pl.when(itself)(here)
        else:
            away()

    def owner_send(phase, buffer, target, chosen):
        for g in chosen:
            for q in range(nq):
                def away():
                    owner_copy(phase, buffer.at[q], target.at[r], q, g).start()

                def here():
                    target[r] = buffer[q]

                owner_each(q, g, away, here)

    holder = lax.rem(r, nj // 2) * 2 + plane
    holds = holder == j

    def far_copy(g):
        return remote(w0, w0, far_send.at[0], far_recv.at[0], r, g * 2 + plane)

    def all_send(phase, src_of, dst):
        for s, p, col in peers:
            remote(src_of(s, p), dst, peer_send.at[phase], peer_recv.at[phase], s, col).start()

    loads["c"].wait()
    loads["x"].wait()
    first = dot_nt(cv[...].reshape(nb, cw), xv[0].astype(BF16))
    asend[...] = first.astype(BF16).reshape(asend.shape)

    if mb < LANES:
        for i in range(nr):
            vall[i, pl.ds(mb, LANES - mb)] = jnp.zeros((LANES - mb, nv), BF16)

    pl.semaphore_wait(barrier, greeted)
    owner_send(0, asend, arecv, groups[:1])
    for s in chips:
        val_copy(s).start()
    loads["v"].wait()
    pass_copy(r).start()

    loads["s"].wait()
    scr = sv[...].astype(F32)
    scr = jnp.concatenate([scr, jnp.zeros((LANES - mb, nb), F32)], axis=0)
    wide = -(-nb // LANES) * LANES
    if wide > nb:
        scr = jnp.concatenate([scr, jnp.zeros((LANES, wide - nb), F32)], axis=1)
    scr = scr.T
    st[...] = scr[:nb].astype(BF16).reshape(st.shape)
    owner_send(1, st, sall, groups[1:] + groups[:1])
    for s in col_peers:
        remote(c_hbm, call.at[:, j], col_send.at[0], col_recv.at[0], r, s).start()

    def screen(w):
        allv = vall[...].reshape(nr * LANES, nv)
        inner = dot_nt(w, allv)
        tile = jnp.concatenate(
            [(sall[i].astype(F32) * inner[:, i * LANES:(i + 1) * LANES]).astype(BF16)
             for i in range(nr)], axis=1)
        return jnp.dot(tile, allv, preferred_element_type=F32).astype(BF16)

    @pl.when(holds)
    def _():
        arrived(arecv.at[pl.ds(0, nr - 1)], own_recv.at[0])
        total = arecv[0].astype(F32)
        for i in range(1, nr):
            total = total + arecv[i].astype(F32)
        w0[...] = total.astype(BF16)
        for g in groups[1:]:
            far_copy(g).start()

    for s in reversed(chips):
        arrived(val_block(s), val_recv.at[s // 2])
        pass_copy(s).start()

    @pl.when(holds)
    def _():
        arrived(sall.at[pl.ds(0, nr - 1)], own_recv.at[1])

    @pl.when(jnp.logical_not(holds))
    def _():
        arrived(sall, own_recv.at[1])
        arrived(w0, far_recv.at[0])

    arrived(vall.at[pl.ds(0, nr // 2), pl.ds(0, mb)], pass_recv.at[0])
    y0 = screen(w0[...])
    ysend0[0] = y0[:, :vh]
    ysend0[1] = y0[:, vh:]
    all_send(0, lambda s, p: ysend0.at[p], yall0.at[me])
    yall0[me] = ysend0[plane]
    for name in ("ev", "ec", "call"):
        loads[name].wait()
    evb[...] = jnp.broadcast_to(evv[...], (LANES, nv)).T
    ec = ecv[:, pl.ds(pl.multiple_of(r * cw, cw), cw)]
    mine = pl.ds(pl.multiple_of(plane * vh, vh), vh)
    b1t[...] = ((ec - evb[mine, :]) * xv[0, mine, :]).T
    arrived(call.at[:, pl.ds(0, nj - 1)], col_recv.at[0])
    condt[...] = call[...].reshape(np * nk, cw).T
    for s in chips:
        val_copy(s).wait_send()
    sent(vall.at[pl.ds(0, nr // 2), pl.ds(0, mb)], pass_send.at[0])
    sent(call.at[:, pl.ds(0, nj - 1)], col_send.at[0])

    @pl.when(holds)
    def _():
        sent(asend.at[pl.ds(0, nq - 1)], own_send.at[0])
        sent(sall.at[pl.ds(0, nr - 1)], own_send.at[1])
        sent(arecv.at[pl.ds(0, nj // 2 - 1)], far_send.at[0])

    @pl.when(jnp.logical_not(holds))
    def _():
        sent(asend, own_send.at[0])
        sent(sall, own_send.at[1])

    arrived(yall0.at[pl.ds(0, np - 1)], peer_recv.at[0])
    k0t = jnp.dot(condt[...], yall0[...].reshape(np * nk, vh), preferred_element_type=F32)
    x1t = (b1t[...] + k0t).astype(BF16)

    cond = call[...].reshape(np * nk, cw)
    esend[...] = jnp.dot(cond, x1t, preferred_element_type=F32).astype(BF16).reshape(esend.shape)
    all_send(1, lambda s, p: esend.at[s * 2 + p], erecv.at[plane * nr + r])
    erecv[plane * nr + r] = esend[me]
    kz0[plane] = k0t.astype(BF16)

    swap = remote(kz0.at[plane], kz0.at[plane], mate_send.at[0], mate_recv.at[0], r, across)
    swap.start()
    sent(yall0.at[pl.ds(0, np - 1)], peer_send.at[0])
    arrived(erecv.at[pl.ds(0, np - 1)], peer_recv.at[1])

    halves = []
    for h in range(2):
        total = erecv[h * nr].astype(F32)
        for i in range(1, nr):
            total = total + erecv[h * nr + i].astype(F32)
        halves.append(total)
    ysend1[...] = screen(jnp.concatenate(halves, axis=1).astype(BF16))
    from_slot = last_recv.at[r // 2 * 2 + plane]

    def cross(s, col):
        return remote(ysend1, yall1.at[me], last_send.at[0], from_slot, s, col)

    def hand(src, p):
        return remote(src, yall1.at[p], hand_send.at[0], hand_recv.at[0], mate, j)

    for s in chips:
        for p, col in planes:
            cross(s, col).start()
    cross(r, across).start()
    hand(ysend1, me).start()
    yall1[me] = ysend1[...]
    arrived(kz0.at[1 - plane], mate_recv.at[0])
    energy = ec - evb[...]
    k0 = jnp.concatenate([kz0[h].astype(F32).T for h in range(2)], axis=0)
    out_ref[0] = energy * (energy * xv[0] + k0)
    swap.wait_send()
    sent(erecv.at[pl.ds(0, np - 1)], peer_send.at[1])
    sources = ([(rows[nr - 2 * k], p) for k in range(1, nr // 2)
                for p in (1 - plane, plane)])
    for s, p in [(r, 1 - plane)] + sources:
        block = yall1.at[s * 2 + p]
        arrived(block, last_recv.at[s // 2 * 2 + p])
        hand(block, s * 2 + p).start()
    arrived(yall1.at[pl.ds(0, nr)], hand_recv.at[0])
    k1t = jnp.dot(condt[...], yall1[...].reshape(np * nk, nv), preferred_element_type=F32)
    out_ref[0] += k1t.T
    sent(yall1.at[pl.ds(0, nr - 1)], last_send.at[0])
    sent(yall1.at[pl.ds(0, nr)], hand_send.at[0])


def fused(nr, nj, trial, screened, val_points, cond_points, eps_val, eps_cond):
    mb, nv = val_points.shape
    nb, cw = cond_points.shape
    np = 2 * nr
    nq = np // nj
    nk = nb // nq
    vh = nv // 2
    ng = nj // 2
    scratch = [
        pltpu.VMEM(trial.shape, F32),
        pltpu.VMEM(screened.shape, BF16),
        pltpu.VMEM((nq, nk, cw), BF16),
        pltpu.VMEM((1, nv), F32),
        pltpu.VMEM((1, eps_cond.shape[0]), F32),
        pltpu.VMEM((nr, LANES, nv), BF16),
        pltpu.VMEM((nq, nk, LANES), BF16),
        pltpu.VMEM((nr, nk, LANES), BF16),
        pltpu.VMEM((nq, nk, nv), BF16),
        pltpu.VMEM((nr, nk, nv), BF16),
        pltpu.VMEM((nq, nj, nk, cw), BF16),
        pltpu.VMEM((nv, LANES), F32),
        pltpu.VMEM((2, nk, vh), BF16),
        pltpu.VMEM((nk, nv), BF16),
        pltpu.VMEM((np, nk, vh), BF16),
        pltpu.VMEM((np, nk, nv), BF16),
        pltpu.VMEM((np, nk, vh), BF16),
        pltpu.VMEM((np, nk, vh), BF16),
        pltpu.VMEM((2, cw, vh), BF16),
        pltpu.VMEM((nk, nv), BF16),
        pltpu.VMEM((cw, vh), F32),
        pltpu.VMEM((cw, np * nk), BF16),
        pltpu.SemaphoreType.DMA((7,)),
        pltpu.SemaphoreType.DMA((2,)),
        pltpu.SemaphoreType.DMA((2,)),
        pltpu.SemaphoreType.DMA((1,)),
        pltpu.SemaphoreType.DMA((1,)),
        pltpu.SemaphoreType.DMA((2,)),
        pltpu.SemaphoreType.DMA((2,)),
        pltpu.SemaphoreType.DMA((1,)),
        pltpu.SemaphoreType.DMA((1,)),
        pltpu.SemaphoreType.DMA((1,)),
        pltpu.SemaphoreType.DMA((1,)),
        pltpu.SemaphoreType.DMA((nr // 2,)),
        pltpu.SemaphoreType.DMA((nr // 2,)),
        pltpu.SemaphoreType.DMA((1,)),
        pltpu.SemaphoreType.DMA((1,)),
        pltpu.SemaphoreType.DMA((1,)),
        pltpu.SemaphoreType.DMA((nr,)),
        pltpu.SemaphoreType.DMA((1,)),
        pltpu.SemaphoreType.DMA((1,)),
    ]
    return pl.pallas_call(
        functools.partial(kernel, nr, nj),
        out_shape=pltpu.VMEM(trial.shape, F32),
        in_specs=[pl.BlockSpec(memory_space=pltpu.HBM)] * 6,
        out_specs=pl.BlockSpec(memory_space=pltpu.VMEM),
        scratch_shapes=scratch,
        compiler_params=pltpu.CompilerParams(
            collective_id=0, has_side_effects=True, vmem_limit_bytes=64 * 2**20 - 2**18),
    )(trial, screened, val_points, cond_points.reshape(nq, nk, cw), eps_val[None], eps_cond[None])


def fits(nr, nj, trial, val_points, cond_points):
    mb, nv = val_points.shape
    nb, cw = cond_points.shape
    if nr % 2 or nj % 2 or (2 * nr) % nj or nb % (2 * nr // nj):
        return False
    nk = nb // (2 * nr // nj)
    return (trial.shape[0] == 1 and cw == LANES and nk % ROWS16 == 0
            and mb % ROWS16 == 0 and mb <= LANES and nv == 2 * LANES)


def general(trial, screened, val_points, cond_points, eps_val, eps_cond):
    cond_full = lax.all_gather(cond_points, "row", axis=1, tiled=True)
    energy_full = eps_cond[None, :] - eps_val[:, None]
    width = trial.shape[2]
    offset = lax.axis_index("row") * width
    x_full = lax.all_gather(trial.astype(BF16), "row", axis=2, tiled=True).astype(trial.dtype)
    xb_full = x_full.astype(BF16)
    x_mine = trial
    for step in range(APPLY):
        pair = jnp.einsum(
            "mv,bvc->bmc", val_points, xb_full, preferred_element_type=F32).astype(BF16)
        inner = jnp.einsum("bmc,nc->bmn", pair, cond_full, preferred_element_type=F32)
        tile = (screened[None] * inner).astype(BF16)
        back = jnp.einsum("bmn,nc->bmc", tile, cond_full, preferred_element_type=F32).astype(BF16)
        part_low = jnp.einsum(
            "mv,bmc->bvc", val_points, back, preferred_element_type=F32).astype(BF16)
        partial_terms = lax.optimization_barrier(part_low).astype(F32)
        kernel_full = lax.psum(partial_terms, ("row", "col"))
        x_full = energy_full[None] * x_full + kernel_full
        xb_full = x_full.astype(BF16)
        x_mine = lax.dynamic_slice_in_dim(x_full, offset, width, 2)
    return x_mine


def solution(mesh):
    nr, nj = mesh.shape["row"], mesh.shape["col"]

    def body(trial, screened, val_points, cond_points, eps_val, eps_cond):
        args = (trial, screened, val_points, cond_points, eps_val, eps_cond)
        if fits(nr, nj, trial, val_points, cond_points):
            return fused(nr, nj, *args)
        return general(*args)

    in_specs = (P(None, None, "row"), P("row", "col"), P("row", None), P("col", "row"), P(), P())
    out_specs = P(None, None, "row")
    return jax.shard_map(body, mesh=mesh, in_specs=in_specs, out_specs=out_specs, check_vma=False)
```

```python
import functools

import jax
import jax.numpy as jnp
from jax import lax
from jax.experimental import pallas as pl
from jax.experimental.pallas import tpu as pltpu
from jax.sharding import PartitionSpec as P

APPLY = 2
LANES = 128
ROWS16 = 16
F32 = jnp.float32
BF16 = jnp.bfloat16
MESH = pl.DeviceIdType.MESH


def dot_nt(a, b):
    return lax.dot_general(a, b, (((1,), (1,)), ((), ())), preferred_element_type=F32)


def wrap(x, n):
    return lax.select(x >= n, x - n, x)


def kernel(nr, nj, x_hbm, s_hbm, v_hbm, c_hbm, ev_hbm, ec_hbm, out_ref,
           xv, sv, cv, evv, ecv, vall, st, sall, asend, arecv, call, evb,
           ysend0, ysend1, yall0, yall1, esend, erecv, kz0, w0, b1t, condt,
           local_sem, own_send, own_recv, col_send, col_recv, peer_send, peer_recv,
           mate_send, mate_recv, far_send, far_recv,
           val_send, val_recv, pass_send, pass_recv,
           last_send, last_recv, hand_send, hand_recv):
    r = lax.axis_index("row")
    j = lax.axis_index("col")
    group, plane = j // 2, lax.rem(j, 2)
    me = r * 2 + plane
    np = nr * 2
    nq = np // nj
    mb, nv = v_hbm.shape
    _, nk, cw = c_hbm.shape
    nb = nq * nk
    vh = nv // 2

    loads = {}

    def load(names):
        for name, src, dst in names:
            loads[name] = pltpu.make_async_copy(src, dst, local_sem.at[len(loads)])
            loads[name].start()

    load([("c", c_hbm, cv), ("x", x_hbm, xv)])
    barrier = pltpu.get_barrier_semaphore()
    across = group * 2 + 1 - plane
    planes = [(1 - plane, across), (plane, j)]
    row_steps = sorted(range(nr), key=lambda k: abs(k - nr // 2))
    rows = {k: wrap(r + k, nr) if k else r for k in range(nr)}
    peers = [(rows[k], p, col) for k in row_steps for p, col in planes if k or col is across]
    chips = [rows[2 * k] for k in range(1, nr // 2)]
    mate = r + 1 - 2 * lax.rem(r, 2)
    col_peers = [wrap(j + k, nj) for k in range(1, nj)]
    far_groups = [wrap(group + k, nj // 2) for k in range(1, nj // 2)]
    for g in far_groups:
        for s in range(nr):
            pl.semaphore_signal(barrier, inc=1, device_id=(s, g * 2 + plane),
                                device_id_type=MESH)
        pl.semaphore_signal(barrier, inc=1, device_id=(r, g * 2 + 1 - plane),
                            device_id_type=MESH)
    for s, p, col in peers:
        pl.semaphore_signal(barrier, inc=1, device_id=(s, col), device_id_type=MESH)
    greeted = np - 1 + (nj // 2 - 1) * (nr + 1)

    load([("v", v_hbm, vall.at[r, pl.ds(0, mb)]), ("s", s_hbm, sv), ("ev", ev_hbm, evv),
          ("ec", ec_hbm, ecv), ("call", c_hbm, call.at[:, j])])

    def remote(src, dst, send_sem, recv_sem, row, col):
        return pltpu.make_async_remote_copy(
            src_ref=src, dst_ref=dst, send_sem=send_sem, recv_sem=recv_sem,
            device_id=(row, col), device_id_type=MESH)

    def arrived(ref, sem):
        remote(ref, ref, col_send.at[0], sem, mate, j).wait_recv()

    def sent(ref, sem):
        remote(ref, ref, sem, col_recv.at[0], mate, j).wait_send()

    def val_block(s):
        return vall.at[s, pl.ds(0, mb)]

    def val_copy(s):
        return remote(v_hbm, val_block(r), val_send.at[s // 2], val_recv.at[r // 2], s, j)

    def pass_copy(s):
        return remote(val_block(s), val_block(s), pass_send.at[0], pass_recv.at[0], mate, j)

    def owner_copy(phase, src, dst, q, g):
        return remote(src, dst, own_send.at[phase], own_recv.at[phase],
                      q * (nj // 2) + group, g * 2 + plane)

    groups = [group] + far_groups

    def owner_each(q, g, away, here):
        if g is groups[0]:
            itself = q * (nj // 2) + group == r
            pl.when(jnp.logical_not(itself))(away)
            if here is not None:
                pl.when(itself)(here)
        else:
            away()

    def owner_send(phase, buffer, target, chosen):
        for g in chosen:
            for q in range(nq):
                def away():
                    owner_copy(phase, buffer.at[q], target.at[r], q, g).start()

                def here():
                    target[r] = buffer[q]

                owner_each(q, g, away, here)

    holder = lax.rem(r, nj // 2) * 2 + plane
    holds = holder == j

    def far_copy(g):
        return remote(w0, w0, far_send.at[0], far_recv.at[0], r, g * 2 + plane)

    def all_send(phase, src_of, dst):
        for s, p, col in peers:
            remote(src_of(s, p), dst, peer_send.at[phase], peer_recv.at[phase], s, col).start()

    loads["c"].wait()
    loads["x"].wait()
    first = dot_nt(cv[...].reshape(nb, cw), xv[0].astype(BF16))
    asend[...] = first.astype(BF16).reshape(asend.shape)

    if mb < LANES:
        for i in range(nr):
            vall[i, pl.ds(mb, LANES - mb)] = jnp.zeros((LANES - mb, nv), BF16)

    loads["s"].wait()
    scr = sv[...].astype(F32)
    scr = jnp.concatenate([scr, jnp.zeros((LANES - mb, nb), F32)], axis=0)
    wide = -(-nb // LANES) * LANES
    if wide > nb:
        scr = jnp.concatenate([scr, jnp.zeros((LANES, wide - nb), F32)], axis=1)
    scr = scr.T
    st[...] = scr[:nb].astype(BF16).reshape(st.shape)

    pl.semaphore_wait(barrier, greeted)
    owner_send(0, asend, arecv, groups[:1])
    for s in chips:
        val_copy(s).start()
    loads["v"].wait()
    pass_copy(r).start()

    owner_send(1, st, sall, groups[1:] + groups[:1])
    for s in col_peers:
        remote(c_hbm, call.at[:, j], col_send.at[0], col_recv.at[0], r, s).start()

    def screen(w):
        allv = vall[...].reshape(nr * LANES, nv)
        inner = dot_nt(w, allv)
        tile = jnp.concatenate(
            [(sall[i].astype(F32) * inner[:, i * LANES:(i + 1) * LANES]).astype(BF16)
             for i in range(nr)], axis=1)
        return jnp.dot(tile, allv, preferred_element_type=F32).astype(BF16)

    @pl.when(holds)
    def _():
        arrived(arecv.at[pl.ds(0, nr - 1)], own_recv.at[0])
        total = arecv[0].astype(F32)
        for i in range(1, nr):
            total = total + arecv[i].astype(F32)
        w0[...] = total.astype(BF16)
        for g in groups[1:]:
            far_copy(g).start()

    for s in reversed(chips):
        arrived(val_block(s), val_recv.at[s // 2])
        pass_copy(s).start()

    @pl.when(holds)
    def _():
        arrived(sall.at[pl.ds(0, nr - 1)], own_recv.at[1])

    @pl.when(jnp.logical_not(holds))
    def _():
        arrived(sall, own_recv.at[1])
        arrived(w0, far_recv.at[0])

    arrived(vall.at[pl.ds(0, nr // 2), pl.ds(0, mb)], pass_recv.at[0])
    y0 = screen(w0[...])
    ysend0[0] = y0[:, :vh]
    ysend0[1] = y0[:, vh:]
    all_send(0, lambda s, p: ysend0.at[p], yall0.at[me])
    yall0[me] = ysend0[plane]
    for name in ("ev", "ec", "call"):
        loads[name].wait()
    evb[...] = jnp.broadcast_to(evv[...], (LANES, nv)).T
    ec = ecv[:, pl.ds(pl.multiple_of(r * cw, cw), cw)]
    mine = pl.ds(pl.multiple_of(plane * vh, vh), vh)
    b1t[...] = ((ec - evb[mine, :]) * xv[0, mine, :]).T
    arrived(call.at[:, pl.ds(0, nj - 1)], col_recv.at[0])
    condt[...] = call[...].reshape(np * nk, cw).T
    for s in chips:
        val_copy(s).wait_send()
    sent(vall.at[pl.ds(0, nr // 2), pl.ds(0, mb)], pass_send.at[0])
    sent(call.at[:, pl.ds(0, nj - 1)], col_send.at[0])

    @pl.when(holds)
    def _():
        sent(asend.at[pl.ds(0, nq - 1)], own_send.at[0])
        sent(sall.at[pl.ds(0, nr - 1)], own_send.at[1])
        sent(arecv.at[pl.ds(0, nj // 2 - 1)], far_send.at[0])

    @pl.when(jnp.logical_not(holds))
    def _():
        sent(asend, own_send.at[0])
        sent(sall, own_send.at[1])

    arrived(yall0.at[pl.ds(0, np - 1)], peer_recv.at[0])
    k0t = jnp.dot(condt[...], yall0[...].reshape(np * nk, vh), preferred_element_type=F32)
    x1t = (b1t[...] + k0t).astype(BF16)

    cond = call[...].reshape(np * nk, cw)
    esend[...] = jnp.dot(cond, x1t, preferred_element_type=F32).astype(BF16).reshape(esend.shape)
    all_send(1, lambda s, p: esend.at[s * 2 + p], erecv.at[plane * nr + r])
    erecv[plane * nr + r] = esend[me]
    kz0[plane] = k0t.astype(BF16)

    swap = remote(kz0.at[plane], kz0.at[plane], mate_send.at[0], mate_recv.at[0], r, across)
    swap.start()
    sent(yall0.at[pl.ds(0, np - 1)], peer_send.at[0])
    arrived(erecv.at[pl.ds(0, np - 1)], peer_recv.at[1])

    halves = []
    for h in range(2):
        total = erecv[h * nr].astype(F32)
        for i in range(1, nr):
            total = total + erecv[h * nr + i].astype(F32)
        halves.append(total)
    ysend1[...] = screen(jnp.concatenate(halves, axis=1).astype(BF16))
    from_slot = last_recv.at[r // 2 * 2 + plane]

    def cross(s, col):
        return remote(ysend1, yall1.at[me], last_send.at[0], from_slot, s, col)

    def hand(src, p):
        return remote(src, yall1.at[p], hand_send.at[0], hand_recv.at[0], mate, j)

    for s in chips:
        for p, col in planes:
            cross(s, col).start()
    cross(r, across).start()
    hand(ysend1, me).start()
    yall1[me] = ysend1[...]
    arrived(kz0.at[1 - plane], mate_recv.at[0])
    energy = ec - evb[...]
    k0 = jnp.concatenate([kz0[h].astype(F32).T for h in range(2)], axis=0)
    out_ref[0] = energy * (energy * xv[0] + k0)
    swap.wait_send()
    sent(erecv.at[pl.ds(0, np - 1)], peer_send.at[1])
    sources = ([(rows[nr - 2 * k], p) for k in range(1, nr // 2)
                for p in (1 - plane, plane)])
    for s, p in [(r, 1 - plane)] + sources:
        block = yall1.at[s * 2 + p]
        arrived(block, last_recv.at[s // 2 * 2 + p])
        hand(block, s * 2 + p).start()
    arrived(yall1.at[pl.ds(0, nr)], hand_recv.at[0])
    k1t = jnp.dot(condt[...], yall1[...].reshape(np * nk, nv), preferred_element_type=F32)
    out_ref[0] += k1t.T
    sent(yall1.at[pl.ds(0, nr - 1)], last_send.at[0])
    sent(yall1.at[pl.ds(0, nr)], hand_send.at[0])


def fused(nr, nj, trial, screened, val_points, cond_points, eps_val, eps_cond):
    mb, nv = val_points.shape
    nb, cw = cond_points.shape
    np = 2 * nr
    nq = np // nj
    nk = nb // nq
    vh = nv // 2
    ng = nj // 2
    scratch = [
        pltpu.VMEM(trial.shape, F32),
        pltpu.VMEM(screened.shape, BF16),
        pltpu.VMEM((nq, nk, cw), BF16),
        pltpu.VMEM((1, nv), F32),
        pltpu.VMEM((1, eps_cond.shape[0]), F32),
        pltpu.VMEM((nr, LANES, nv), BF16),
        pltpu.VMEM((nq, nk, LANES), BF16),
        pltpu.VMEM((nr, nk, LANES), BF16),
        pltpu.VMEM((nq, nk, nv), BF16),
        pltpu.VMEM((nr, nk, nv), BF16),
        pltpu.VMEM((nq, nj, nk, cw), BF16),
        pltpu.VMEM((nv, LANES), F32),
        pltpu.VMEM((2, nk, vh), BF16),
        pltpu.VMEM((nk, nv), BF16),
        pltpu.VMEM((np, nk, vh), BF16),
        pltpu.VMEM((np, nk, nv), BF16),
        pltpu.VMEM((np, nk, vh), BF16),
        pltpu.VMEM((np, nk, vh), BF16),
        pltpu.VMEM((2, cw, vh), BF16),
        pltpu.VMEM((nk, nv), BF16),
        pltpu.VMEM((cw, vh), F32),
        pltpu.VMEM((cw, np * nk), BF16),
        pltpu.SemaphoreType.DMA((7,)),
        pltpu.SemaphoreType.DMA((2,)),
        pltpu.SemaphoreType.DMA((2,)),
        pltpu.SemaphoreType.DMA((1,)),
        pltpu.SemaphoreType.DMA((1,)),
        pltpu.SemaphoreType.DMA((2,)),
        pltpu.SemaphoreType.DMA((2,)),
        pltpu.SemaphoreType.DMA((1,)),
        pltpu.SemaphoreType.DMA((1,)),
        pltpu.SemaphoreType.DMA((1,)),
        pltpu.SemaphoreType.DMA((1,)),
        pltpu.SemaphoreType.DMA((nr // 2,)),
        pltpu.SemaphoreType.DMA((nr // 2,)),
        pltpu.SemaphoreType.DMA((1,)),
        pltpu.SemaphoreType.DMA((1,)),
        pltpu.SemaphoreType.DMA((1,)),
        pltpu.SemaphoreType.DMA((nr,)),
        pltpu.SemaphoreType.DMA((1,)),
        pltpu.SemaphoreType.DMA((1,)),
    ]
    return pl.pallas_call(
        functools.partial(kernel, nr, nj),
        out_shape=pltpu.VMEM(trial.shape, F32),
        in_specs=[pl.BlockSpec(memory_space=pltpu.HBM)] * 6,
        out_specs=pl.BlockSpec(memory_space=pltpu.VMEM),
        scratch_shapes=scratch,
        compiler_params=pltpu.CompilerParams(
            collective_id=0, has_side_effects=True, vmem_limit_bytes=64 * 2**20 - 2**18),
    )(trial, screened, val_points, cond_points.reshape(nq, nk, cw), eps_val[None], eps_cond[None])


def fits(nr, nj, trial, val_points, cond_points):
    mb, nv = val_points.shape
    nb, cw = cond_points.shape
    if nr % 2 or nj % 2 or (2 * nr) % nj or nb % (2 * nr // nj):
        return False
    nk = nb // (2 * nr // nj)
    return (trial.shape[0] == 1 and cw == LANES and nk % ROWS16 == 0
            and mb % ROWS16 == 0 and mb <= LANES and nv == 2 * LANES)


def general(trial, screened, val_points, cond_points, eps_val, eps_cond):
    cond_full = lax.all_gather(cond_points, "row", axis=1, tiled=True)
    energy_full = eps_cond[None, :] - eps_val[:, None]
    width = trial.shape[2]
    offset = lax.axis_index("row") * width
    x_full = lax.all_gather(trial.astype(BF16), "row", axis=2, tiled=True).astype(trial.dtype)
    xb_full = x_full.astype(BF16)
    x_mine = trial
    for step in range(APPLY):
        pair = jnp.einsum(
            "mv,bvc->bmc", val_points, xb_full, preferred_element_type=F32).astype(BF16)
        inner = jnp.einsum("bmc,nc->bmn", pair, cond_full, preferred_element_type=F32)
        tile = (screened[None] * inner).astype(BF16)
        back = jnp.einsum("bmn,nc->bmc", tile, cond_full, preferred_element_type=F32).astype(BF16)
        part_low = jnp.einsum(
            "mv,bmc->bvc", val_points, back, preferred_element_type=F32).astype(BF16)
        partial_terms = lax.optimization_barrier(part_low).astype(F32)
        kernel_full = lax.psum(partial_terms, ("row", "col"))
        x_full = energy_full[None] * x_full + kernel_full
        xb_full = x_full.astype(BF16)
        x_mine = lax.dynamic_slice_in_dim(x_full, offset, width, 2)
    return x_mine


def solution(mesh):
    nr, nj = mesh.shape["row"], mesh.shape["col"]

    def body(trial, screened, val_points, cond_points, eps_val, eps_cond):
        args = (trial, screened, val_points, cond_points, eps_val, eps_cond)
        if fits(nr, nj, trial, val_points, cond_points):
            return fused(nr, nj, *args)
        return general(*args)

    in_specs = (P(None, None, "row"), P("row", "col"), P("row", None), P("col", "row"), P(), P())
    out_specs = P(None, None, "row")
    return jax.shard_map(body, mesh=mesh, in_specs=in_specs, out_specs=out_specs, check_vma=False)
```
